128 devices in a mesh: ctx: 32 (over z, y, x_lo), tp: 4 (over x_hi, core).
Axes of the slice: x: 4 (x_hi: 2, x_lo: 2; x = x_hi * 2 + x_lo), y: 4, z: 4, core: 2. Of those that a mesh axis runs over, the one named last changes fastest.
Arguments:
- queries: bfloat16 [512, 2, 6144], P('ctx', None, 'tp'), may hold values from -6 to 6
- new_keys: bfloat16 [512, 2, 1024], P('ctx', None, 'tp'), may hold values from -6 to 6
- new_values: bfloat16 [512, 2, 1024], P('ctx', None, 'tp'), may hold values from -18 to 18
- cached_key_rows: bfloat16 [16384, 2, 1024], P('ctx', None, 'tp'), may hold values from -6 to 6
- cache_values: bfloat16 [16384, 2, 1024], P('ctx', None, 'tp'), may hold values from -18 to 18
- cache_lengths: int32 [2], replicated, may hold values from 1 to 16384, as said below
- norm_gain: bfloat16 [6144], P('tp'), may hold values from 0.25 to 1.75
- routes: int32 [512, 2, 2], P('ctx'), may hold values from 0 to 7, all different within a row; in each aligned block of 32 rows (0 to 31, 32 to 63, ..., all dimensions but the last counted through in order) at most 16 rows name the same one
- gates: float32 [512, 2, 2], P('ctx'), may hold values from 0.2 to 1
- gate_proj: bfloat16 [32, 6144, 2048], P('ctx', None, 'tp'), may hold values from -0.078125 to 0.078125
- up_proj: bfloat16 [32, 6144, 2048], P('ctx', None, 'tp'), may hold values from -0.078125 to 0.078125
- down_proj: bfloat16 [32, 2048, 6144], P('ctx', None, 'tp'), may hold values from -0.0625 to 0.0625
Outputs:
- normed: float32 [512, 2, 6144], P('ctx', None, 'tp')
- moe_out: float32 [512, 2, 6144], P('ctx', None, 'tp')
The draws below stay inside these ranges and needn't reach their ends.
Inputs may be any that keep to these rules, and one draw needn't show every extreme that they name: `routes`: in the tokens of one index of ctx (aligned blocks of 32 tokens) no expert is named more than 16 times, a bound that some block reaches; the 2 experts of a token differ. `cache_lengths`: at least one sequence has all 16384 slots filled.
All inputs are finite; a program needn't handle non-finite values.
Results may differ from the reference program's by a relative error of at most 0.02.
Values may be sent and summed in bfloat16 or wider, within the bound.
No kernel may reach another device: no remote copies, remote signals or barrier semaphores. Data moves between devices by JAX's collectives and lax.ppermute only.
A program may use at most 128 MiB of HBM per device.

```python
import math
import jax
import jax.numpy as jnp
import numpy as np
from jax import lax

QUERY_HEADS = 48
KEY_VALUE_HEADS = 8
HEAD_SIZE = 128
D = 6144
EXPERTS = 8
TOPK = 2
FF = 8192
SEQUENCE_COUNT = 2
NEW_DEV = 16
NEW_TOKENS = 512
CACHE_SLOTS = 16384
GROUP = 4
CAP = 16
N_CTX = 32


def truncated_gaussian(key, dimensions):
    return jnp.clip(jax.random.normal(key, dimensions, jnp.float32), -6.0, 6.0)


def head_rescaled(base_value):
    multiplier = 3.0 ** (jnp.arange(KEY_VALUE_HEADS, dtype=jnp.float32) / max(KEY_VALUE_HEADS - 1, 1))
    return (base_value * multiplier[:, None]).reshape(base_value.shape[0], SEQUENCE_COUNT, KEY_VALUE_HEADS * HEAD_SIZE).astype(jnp.bfloat16)


def draw_queries(key, part):
    key = jax.random.fold_in(key, 3)
    base_value = truncated_gaussian(key, (NEW_TOKENS, SEQUENCE_COUNT, QUERY_HEADS, HEAD_SIZE))
    return base_value.reshape(NEW_TOKENS, SEQUENCE_COUNT, QUERY_HEADS * HEAD_SIZE).astype(jnp.bfloat16)


def draw_new_keys(key, part):
    key = jax.random.fold_in(key, 4)
    base_value = truncated_gaussian(key, (NEW_TOKENS, SEQUENCE_COUNT, KEY_VALUE_HEADS, HEAD_SIZE))
    return base_value.reshape(NEW_TOKENS, SEQUENCE_COUNT, KEY_VALUE_HEADS * HEAD_SIZE).astype(jnp.bfloat16)


def draw_new_values(key, part):
    key = jax.random.fold_in(key, 5)
    return head_rescaled(truncated_gaussian(key, (NEW_TOKENS, SEQUENCE_COUNT, KEY_VALUE_HEADS, HEAD_SIZE)))


def draw_cache_values(key, part):
    key = jax.random.fold_in(key, 6)
    return head_rescaled(truncated_gaussian(key, (CACHE_SLOTS, SEQUENCE_COUNT, KEY_VALUE_HEADS, HEAD_SIZE)))


def draw_cache_lengths(key, part):
    key = jax.random.fold_in(key, 7)
    first, second = jax.random.split(key)
    others = jax.random.randint(first, (SEQUENCE_COUNT,), 1, CACHE_SLOTS + 1)
    full_at = jax.random.randint(second, (), 0, SEQUENCE_COUNT)
    return jnp.where(jnp.arange(SEQUENCE_COUNT) == full_at, CACHE_SLOTS, others).astype(jnp.int32)


def level_of(key, extent, cuts, low, largest):
    def one(dim, parts):
        heights = jax.random.uniform(jax.random.fold_in(jax.random.fold_in(key, 6), dim), (parts,), jnp.float32, low / len(cuts), largest / len(cuts))
        return jnp.repeat(jnp.exp(heights), extent[dim] // parts).reshape((-1,) + (1,) * (len(extent) - dim - 1))

    factor_of = one(*cuts[0])
    for cut in cuts[1:]:
        factor_of = factor_of * one(*cut)
    return factor_of


def deal_out(rng, own, number, rows, number_of, top, reach, skew):
    ranking = jax.random.permutation(rng, number_of)
    crowded, usual = load_shares(number_of, rows * top, reach, skew, True), load_shares(number_of, rows * top, reach, skew, False)
    places = jnp.arange(number_of)

    def named(sizes, offset_by):
        used = int((sizes > 0).sum())
        fixed = max(1, used // 4)
        shifted = fixed + (places - fixed + offset_by * (used - fixed)) % max(1, number_of - fixed)
        return jnp.zeros((number_of,), jnp.int32).at[ranking[jnp.where(places < fixed, places, shifted)]].set(jnp.asarray(sizes, jnp.int32))

    sizes = jnp.where(number % 4 == 0, named(crowded, number // 4), named(usual, number - number // 4 - 1))
    mixed = jax.random.permutation(jax.random.fold_in(own, 3), number_of)
    giver, receiver = mixed[0:number_of // 2 * 2:2], mixed[1:number_of // 2 * 2:2]
    room = jnp.minimum(sizes[giver] - 1, reach - sizes[receiver]) // 2
    room = jnp.where((giver == ranking[0]) | (receiver == ranking[0]) | (sizes[receiver] == 0), 0, jnp.maximum(room, 0))
    shifted = jax.random.randint(jax.random.fold_in(own, 4), (number_of // 2,), 0, 1 << 20) % (room + 1)
    sizes = sizes.at[giver].add(-shifted).at[receiver].add(shifted)
    members = jnp.searchsorted(jnp.cumsum(sizes), jnp.arange(rows * top), side="right").astype(jnp.int32)
    grid = members.reshape(top, rows).T
    grid = grid[jax.random.permutation(jax.random.fold_in(own, 1), rows)]
    offset_by = jax.random.randint(jax.random.fold_in(own, 2), (rows, 1), 0, top)
    return jnp.take_along_axis(grid, (jnp.arange(top)[None, :] + offset_by) % top, axis=1)


def load_shares(number_of, total, reach, slope, full):
    loads = [(1 << 20) // math.isqrt(grade ** slope) + 1 for grade in range(1, number_of + 1)]
    largest = reach if full else min(reach, max(-(-total // number_of), total * loads[0] // sum(loads)))
    least = 1 if total - largest >= number_of - 1 else 0
    given, spare = [largest] + [least] * (number_of - 1), total - largest - least * (number_of - 1)
    while spare > 0:
        movable = [i for i in range(1, number_of) if given[i] < largest] or [i for i in range(1, number_of) if given[i] < reach]
        mass, budget = sum([loads[i] for i in movable]), spare
        for i in movable:
            extra = min(reach - given[i], max(1, budget * loads[i] // mass), spare)
            given[i] = given[i] + extra
            spare = spare - extra
    return np.array(given)


def scatter_about(stream_key, dims, deviation, reach, pieces=(), kind=jnp.bfloat16):
    entries = deviation * jax.random.normal(stream_key, dims, jnp.float32)
    if pieces:
        entries = entries * level_of(stream_key, dims, pieces, -0.22, 0.18)
    return jnp.clip(entries, -reach, reach).astype(kind)


def setup_inputs(seed: int = 0) -> dict:
    keys = jax.random.split(jax.random.key(seed), 13)
    queries = draw_queries(jax.random.fold_in(keys[12], 71), 0)
    new_keys = draw_new_keys(jax.random.fold_in(keys[12], 71), 0)
    new_values = draw_new_values(jax.random.fold_in(keys[12], 71), 0)
    cached_key_rows = scatter_about(keys[3], (CACHE_SLOTS, SEQUENCE_COUNT, KEY_VALUE_HEADS * HEAD_SIZE), 1.0, 6.0, ((0, 32), (2, 4)))
    cache_values = draw_cache_values(jax.random.fold_in(keys[12], 71), 0)
    cache_lengths = draw_cache_lengths(jax.random.fold_in(keys[12], 71), 0)
    norm_gain = jnp.clip(1.0 + 0.15 * jax.random.normal(keys[6], (D,), jnp.float32), 0.25, 1.75).astype(jnp.bfloat16)
    routes_keys = jax.random.split(jax.random.fold_in(keys[7], 1), NEW_TOKENS * SEQUENCE_COUNT // (NEW_DEV * SEQUENCE_COUNT))
    routes_turns = jax.random.permutation(jax.random.fold_in(keys[7], 3), NEW_TOKENS * SEQUENCE_COUNT // (NEW_DEV * SEQUENCE_COUNT))
    routes = jax.vmap(lambda own, number: deal_out(jax.random.fold_in(keys[7], 2), own, number, NEW_DEV * SEQUENCE_COUNT, EXPERTS, TOPK, CAP, 2))(routes_keys, routes_turns).reshape((NEW_TOKENS, SEQUENCE_COUNT, TOPK))
    gates = jnp.clip(0.2 + 0.8 * jax.random.uniform(keys[8], (NEW_TOKENS, SEQUENCE_COUNT, TOPK), jnp.float32) ** level_of(keys[8], (NEW_TOKENS, SEQUENCE_COUNT, TOPK), ((0, 32),), -0.2, 0.2), 0.2, 1.0)
    gate_proj = scatter_about(keys[9], (EXPERTS * GROUP, D, FF // GROUP), D ** -0.5, 0.078125, ((0, 32), (2, 4)))
    up_proj = scatter_about(keys[10], (EXPERTS * GROUP, D, FF // GROUP), D ** -0.5, 0.078125, ((0, 32), (2, 4)))
    down_proj = scatter_about(keys[11], (EXPERTS * GROUP, FF // GROUP, D), FF ** -0.5, 0.0625, ((0, 32), (2, 4)))
    return dict(queries=queries, new_keys=new_keys, new_values=new_values, cached_key_rows=cached_key_rows, cache_values=cache_values, cache_lengths=cache_lengths, norm_gain=norm_gain, routes=routes, gates=gates, gate_proj=gate_proj, up_proj=up_proj, down_proj=down_proj)


FLOOR = -1e+30
EPS = 1e-05

def attend_group(query, key_group, value_group, alive):
    scores = jnp.einsum('prd,kd->rpk', query, key_group) * (1.0 / math.sqrt(HEAD_SIZE))
    masked = jnp.where(alive[None], scores, FLOOR)
    rowmax = lax.optimization_barrier(jnp.max(masked, axis=-1, keepdims=True))
    expo = jnp.where(alive[None], jnp.exp(masked - rowmax), 0.0)
    total = lax.optimization_barrier(jnp.sum(expo, axis=-1))
    probs = lax.optimization_barrier(expo.astype(jnp.bfloat16)).astype(jnp.float32)
    mixed = jnp.einsum('rpk,kd->prd', probs, value_group)
    return mixed / jnp.transpose(total)[:, :, None]

def attend_sequence(query_sequence, key_sequence, value_sequence, length):
    replicate = QUERY_HEADS // KEY_VALUE_HEADS
    slots = jnp.arange(CACHE_SLOTS + NEW_TOKENS)
    position = jnp.arange(NEW_TOKENS)
    alive = jnp.where(slots[None, :] < CACHE_SLOTS, slots[None, :] < length, slots[None, :] - CACHE_SLOTS <= position[:, None])
    query_clustered = jnp.transpose(query_sequence.astype(jnp.float32).reshape(NEW_TOKENS, KEY_VALUE_HEADS, replicate, HEAD_SIZE), (1, 0, 2, 3))
    key_clustered = jnp.transpose(key_sequence.astype(jnp.float32).reshape(CACHE_SLOTS + NEW_TOKENS, KEY_VALUE_HEADS, HEAD_SIZE), (1, 0, 2))
    value_clustered = jnp.transpose(value_sequence.astype(jnp.float32).reshape(CACHE_SLOTS + NEW_TOKENS, KEY_VALUE_HEADS, HEAD_SIZE), (1, 0, 2))

    def one_head(items):
        return attend_group(items[0], items[1], items[2], alive)
    heads = lax.map(one_head, (query_clustered, key_clustered, value_clustered))
    return jnp.transpose(heads, (1, 0, 2, 3)).reshape(NEW_TOKENS, QUERY_HEADS * HEAD_SIZE)

def mixture(token_rows, route_rows, gate_rows, gate_proj, up_proj, down_proj):
    group = N_CTX // EXPERTS
    block = FF // group
    limit = N_CTX * CAP
    step_rows = math.gcd(128, limit)
    gate_all = gate_proj.reshape(EXPERTS, group, D, block)
    up_all = up_proj.reshape(EXPERTS, group, D, block)
    down_all = down_proj.reshape(EXPERTS, group, block, D)

    def per_expert(carried, items):
        expert, gate_blocks, up_blocks, down_blocks = items
        gate_full = jnp.transpose(gate_blocks, (1, 0, 2)).reshape(D, FF)
        up_full = jnp.transpose(up_blocks, (1, 0, 2)).reshape(D, FF)
        hit = route_rows == expert
        weight = lax.optimization_barrier(jnp.sum(jnp.where(hit, gate_rows, 0.0), axis=1))
        chosen = jnp.any(hit, axis=1)
        indices = jnp.nonzero(chosen, size=limit, fill_value=0)[0].astype(jnp.int32)
        count = jnp.sum(chosen.astype(jnp.int32))

        def per_block(number, running):
            start = (number * step_rows).astype(jnp.int32)
            picked = lax.dynamic_slice_in_dim(indices, start, step_rows)
            inputs = token_rows[picked]
            gate_val = jnp.dot(inputs, gate_full, preferred_element_type=jnp.float32)
            up_val = jnp.dot(inputs, up_full, preferred_element_type=jnp.float32)
            hidden = (jax.nn.silu(gate_val) * up_val).astype(jnp.bfloat16)
            summed = jnp.zeros((step_rows, D), jnp.float32)
            for part_index in range(group):
                piece = hidden[:, part_index * block:(part_index + 1) * block]
                summed = summed + jnp.dot(piece, down_blocks[part_index], preferred_element_type=jnp.float32)
            valid = start + jnp.arange(step_rows) < count
            contribution = jnp.where(valid[:, None], weight[picked][:, None] * summed, 0.0)
            return running.at[picked].add(contribution)
        blocks_used = ((count + step_rows - 1) // step_rows).astype(jnp.int32)
        carried = lax.fori_loop(jnp.int32(0), blocks_used, per_block, carried)
        return (carried, None)
    start_total = jnp.zeros((token_rows.shape[0], D), jnp.float32)
    result, _ = lax.scan(per_expert, start_total, (jnp.arange(EXPERTS, dtype=jnp.int32), gate_all, up_all, down_all))
    return result

def reference(queries, new_keys, new_values, cached_key_rows, cache_values, cache_lengths, norm_gain, routes, gates, gate_proj, up_proj, down_proj):
    attended_list = []
    for sequence in range(SEQUENCE_COUNT):
        key_sequence = jnp.concatenate([cached_key_rows[:, sequence], new_keys[:, sequence]], axis=0)
        value_sequence = jnp.concatenate([cache_values[:, sequence], new_values[:, sequence]], axis=0)
        output = attend_sequence(queries[:, sequence], key_sequence, value_sequence, cache_lengths[sequence])
        attended_list.append(output.astype(jnp.float32))
    wide = jnp.stack(attended_list, axis=1)
    inverse = lax.rsqrt(lax.optimization_barrier(jnp.mean(wide * wide, axis=-1, keepdims=True)) + EPS)
    normed = wide * inverse * norm_gain.astype(jnp.float32)
    normed_bf = normed.astype(jnp.bfloat16)
    moe = mixture(normed_bf.reshape(NEW_TOKENS * SEQUENCE_COUNT, D), routes.reshape(NEW_TOKENS * SEQUENCE_COUNT, TOPK), gates.reshape(NEW_TOKENS * SEQUENCE_COUNT, TOPK), gate_proj, up_proj, down_proj)
    return (normed, moe.reshape(NEW_TOKENS, SEQUENCE_COUNT, D))
```

```python
import math

import jax
import jax.numpy as jnp
from jax import lax
from jax.experimental import pallas as pl
from jax.experimental.pallas import tpu as pltpu
from jax.sharding import Mesh
from jax.sharding import PartitionSpec as P

HEAD_SIZE = 128
EXPERTS = 8
TOPK = 2
CAP = 16
EPS = 1e-05
DEAD = -1e30
LANES = 128
VMEM_LIMIT = 50 * 1024 * 1024

BF16 = jnp.bfloat16
F32 = jnp.float32


def attention_kernel(
    info_ref, q_ref, mine_ref, theirs_ref, out_ref, keys_ref, values_ref, causal_ref, lse_ref, *, chunks
):
    sequence = pl.program_id(0)
    head = pl.program_id(1)
    heads = pl.num_programs(1)
    sources, _, own_rows, _ = q_ref.shape
    rows = sources * own_rows
    count = mine_ref.shape[2]
    padded = keys_ref.shape[0]
    cache = count - own_rows
    length = info_ref[sequence]
    own = info_ref[2]
    other = info_ref[3]
    first = 2 * own_rows * info_ref[4]
    multiplier = 1.0 / math.sqrt(HEAD_SIZE)

    @pl.when(head == 0)
    def _():
        row = lax.broadcasted_iota(jnp.int32, (padded, LANES), 0)
        lane = lax.broadcasted_iota(jnp.int32, (padded, LANES), 1)
        second = row >= count
        index = jnp.where(second, row - count, row)
        index = jnp.where(row >= 2 * count, cache, index)
        owner = jnp.where(second, other, own)
        is_cache = index < cache
        cache_dead = is_cache & (owner * cache + index >= length)
        dead = (lane == 2 * own_rows) & (cache_dead | (row >= 2 * count))
        late = (
            (lane == owner * own_rows - first + index - cache)
            & jnp.logical_not(is_cache)
            & (row < 2 * count)
        )
        bias = jnp.where(dead | late, DEAD, 0.0).astype(BF16)
        keys_ref[:, LANES:] = bias
        values_ref[:, LANES:] = jnp.ones((padded, LANES), BF16)
        keys_ref[:count, :LANES] = mine_ref[0, 0]
        values_ref[:count, :LANES] = mine_ref[1, 0]
        keys_ref[count : 2 * count, :LANES] = theirs_ref[0, 0]
        values_ref[count : 2 * count, :LANES] = theirs_ref[1, 0]
        keys_ref[2 * count :, :LANES] = jnp.zeros((padded - 2 * count, LANES), BF16)
        values_ref[2 * count :, :LANES] = jnp.zeros((padded - 2 * count, LANES), BF16)
        position = lax.broadcasted_iota(jnp.int32, (rows, LANES), 0)
        token = lax.broadcasted_iota(jnp.int32, (rows, LANES), 1)
        blocked = ((token < 2 * own_rows) & (position < first + token)) | (token == 2 * own_rows)
        causal_ref[...] = jnp.where(blocked, 1.0, 0.0).astype(BF16)
        lse_ref[...] = jnp.zeros_like(lse_ref)

    size = rows // chunks
    group = sources // chunks
    for chunk in range(chunks):
        span = slice(chunk * size, (chunk + 1) * size)
        query = q_ref[chunk * group : (chunk + 1) * group, 0].reshape(size, HEAD_SIZE)
        wide = jnp.concatenate([query, causal_ref[span]], axis=1)
        scores = lax.dot_general(
            wide, keys_ref[...], (((1,), (1,)), ((), ())), preferred_element_type=F32
        )
        top = jnp.max(scores, axis=1, keepdims=True)
        expo = jnp.exp2((scores - top) * (multiplier * math.log2(math.e)))
        mixed = jnp.dot(expo.astype(BF16), values_ref[...], preferred_element_type=F32)
        total = mixed[:, LANES:]
        result = mixed[:, :LANES] / total
        lse = top * multiplier + jnp.log(total)
        pairs = group // 2
        out_ref[chunk * pairs : (chunk + 1) * pairs, 0, :, pl.ds(head * HEAD_SIZE, HEAD_SIZE)] = (
            result.astype(BF16).reshape(pairs, 2 * own_rows, HEAD_SIZE)
        )
        lane = lax.broadcasted_iota(jnp.int32, (size, LANES), 1)
        lse_ref[span] = jnp.where((lane % 8 == head) & (lane < 24), lse, lse_ref[span])

    @pl.when(head == heads - 1)
    def _():
        value = lse_ref[...]
        lane = lax.broadcasted_iota(jnp.int32, (rows, LANES), 1)
        high = value.astype(BF16).astype(F32)
        middle = (value - high).astype(BF16).astype(F32)
        low = value - high - middle
        packed = jnp.where(lane < 8, high, jnp.where(lane < 16, middle, low)).astype(BF16)
        out_ref[:, 0, :, pl.ds(heads * HEAD_SIZE, LANES)] = packed.reshape(
            sources // 2, 2 * own_rows, LANES
        )


def attend(info, queries, mine, theirs, chunks=2):
    sources, sequences, own_rows, width = queries.shape
    heads = width // HEAD_SIZE
    count = mine.shape[2]
    padded = -(-2 * count // LANES) * LANES
    rows = sources * own_rows
    return pl.pallas_call(
        lambda *refs: attention_kernel(*refs, chunks=chunks),
        grid_spec=pltpu.PrefetchScalarGridSpec(
            num_scalar_prefetch=1,
            grid=(sequences, heads),
            in_specs=[
                pl.BlockSpec((sources, 1, own_rows, HEAD_SIZE), lambda s, h, i: (0, s, 0, h)),
                pl.BlockSpec((2, 1, count, HEAD_SIZE), lambda s, h, i: (0, s, 0, 0)),
                pl.BlockSpec((2, 1, count, HEAD_SIZE), lambda s, h, i: (0, s, 0, 0)),
            ],
            out_specs=pl.BlockSpec(
                (sources // 2, 1, 2 * own_rows, width + LANES), lambda s, h, i: (0, s, 0, 0)
            ),
            scratch_shapes=[
                pltpu.VMEM((padded, 2 * LANES), BF16),
                pltpu.VMEM((padded, 2 * LANES), BF16),
                pltpu.VMEM((rows, LANES), BF16),
                pltpu.VMEM((rows, LANES), F32),
            ],
        ),
        out_shape=jax.ShapeDtypeStruct(
            (sources // 2, sequences, 2 * own_rows, width + LANES), BF16
        ),
        compiler_params=pltpu.CompilerParams(vmem_limit_bytes=VMEM_LIMIT),
        name="attend",
    )(info, queries, mine, theirs)


def merge_kernel(got_ref, out_ref, square_ref):
    sources, _, rows, wide = got_ref.shape
    width = wide - LANES
    parts = got_ref[:, 0, :, width:].astype(F32).reshape(sources * rows, LANES)
    lse = parts + pltpu.roll(parts, LANES - 8, 1) + pltpu.roll(parts, LANES - 16, 1)
    lse = lse.reshape(sources, rows, LANES)
    weight = jnp.exp(lse - jnp.max(lse, axis=0, keepdims=True))
    weight = weight / jnp.sum(weight, axis=0, keepdims=True)
    square = jnp.zeros((rows, 1), F32)
    for head in range(width // HEAD_SIZE):
        lanes = slice(head * HEAD_SIZE, (head + 1) * HEAD_SIZE)
        merged = jnp.zeros((rows, HEAD_SIZE), F32)
        for source in range(sources):
            merged = merged + weight[source, :, head : head + 1] * got_ref[
                source, 0, :, lanes
            ].astype(F32)
        out_ref[0, :, lanes] = merged
        square = square + jnp.sum(merged * merged, axis=1, keepdims=True)
    square_ref[0] = jnp.broadcast_to(square, (rows, LANES))


def merge(got):
    sources, sequences, rows, wide = got.shape
    width = wide - LANES
    return pl.pallas_call(
        merge_kernel,
        grid=(sequences,),
        in_specs=[pl.BlockSpec((sources, 1, rows, wide), lambda s: (0, s, 0, 0))],
        out_specs=[
            pl.BlockSpec((1, rows, width), lambda s: (s, 0, 0)),
            pl.BlockSpec((1, rows, LANES), lambda s: (s, 0, 0)),
        ],
        out_shape=[
            jax.ShapeDtypeStruct((sequences, rows, width), F32),
            jax.ShapeDtypeStruct((sequences, rows, LANES), F32),
        ],
        compiler_params=pltpu.CompilerParams(vmem_limit_bytes=VMEM_LIMIT),
        name="merge",
    )(got)


def hidden_kernel(info_ref, near_ref, far_ref, gate_ref, up_ref, out_ref, gate_sum, up_sum):
    step = pl.program_id(0)
    steps = pl.num_programs(0)

    @pl.when(step == 0)
    def _():
        gate_sum[...] = jnp.zeros_like(gate_sum)
        up_sum[...] = jnp.zeros_like(up_sum)

    def add(rows_ref):
        rows = rows_ref[:, 0].reshape(gate_sum.shape[0], rows_ref.shape[3])
        gate_sum[...] += jnp.dot(rows, gate_ref[0], preferred_element_type=F32)
        up_sum[...] += jnp.dot(rows, up_ref[0], preferred_element_type=F32)

    @pl.when(step < steps // 2)
    def _():
        add(near_ref)

    @pl.when(step >= steps // 2)
    def _():
        add(far_ref)

    @pl.when(step == steps - 1)
    def _():
        gate = gate_sum[...]
        out_ref[...] = (gate / (1.0 + jnp.exp(-gate)) * up_sum[...]).astype(BF16)


def hidden_units(info, near, far, gate_proj, up_proj):
    sources, quarters, rows, width = near.shape
    tokens = sources * rows
    units = gate_proj.shape[2]

    def weight_block(step, info):
        quarter = step % quarters
        core = jnp.where(step < quarters, info[0], 1 - info[0])
        return (0, ((quarter % 2) * 2 + core) * 2 + quarter // 2, 0)

    return pl.pallas_call(
        hidden_kernel,
        grid_spec=pltpu.PrefetchScalarGridSpec(
            num_scalar_prefetch=1,
            grid=(2 * quarters,),
            in_specs=[
                pl.BlockSpec(
                    (sources, 1, rows, width),
                    lambda k, i: (0, jnp.minimum(k, quarters - 1), 0, 0),
                ),
                pl.BlockSpec(
                    (sources, 1, rows, width),
                    lambda k, i: (0, jnp.maximum(k - quarters, 0), 0, 0),
                ),
                pl.BlockSpec((1, width, units), weight_block),
                pl.BlockSpec((1, width, units), weight_block),
            ],
            out_specs=pl.BlockSpec((tokens, units), lambda k, i: (0, 0)),
            scratch_shapes=[pltpu.VMEM((tokens, units), F32), pltpu.VMEM((tokens, units), F32)],
        ),
        out_shape=jax.ShapeDtypeStruct((tokens, units), BF16),
        compiler_params=pltpu.CompilerParams(vmem_limit_bytes=VMEM_LIMIT),
        name="hidden_units",
    )(info, near, far, gate_proj, up_proj)


def down_kernel(info_ref, a_ref, b_ref, c_ref, d_ref, down_ref, out_ref):
    mine = info_ref[1]
    units = a_ref.shape[1]
    total = None
    for index, rows_ref in enumerate((a_ref, b_ref, c_ref, d_ref)):
        start = pl.multiple_of((mine ^ index) * units, units)
        term = jnp.dot(
            rows_ref[...], down_ref[0, pl.ds(start, units), :], preferred_element_type=F32
        )
        total = term if total is None else total + term
    out_ref[...] = total.astype(BF16)


def block_outputs(info, hiddens, down_proj):
    tokens, units = hiddens[0].shape
    depth, columns = down_proj.shape[1:]
    tile = 512
    return pl.pallas_call(
        down_kernel,
        grid_spec=pltpu.PrefetchScalarGridSpec(
            num_scalar_prefetch=1,
            grid=(columns // tile,),
            in_specs=[pl.BlockSpec((tokens, units), lambda n, i: (0, 0)) for _ in hiddens]
            + [pl.BlockSpec((1, depth, tile), lambda n, i: (0, 0, n))],
            out_specs=pl.BlockSpec((tokens, tile), lambda n, i: (0, n)),
        ),
        out_shape=jax.ShapeDtypeStruct((tokens, columns), BF16),
        compiler_params=pltpu.CompilerParams(vmem_limit_bytes=VMEM_LIMIT),
        name="block_outputs",
    )(info, *hiddens, down_proj)


def swap(array, axis):
    return lax.ppermute(array, axis, [(0, 1), (1, 0)])


def on_device(
    queries,
    new_keys,
    new_values,
    cached_key_rows,
    cache_values,
    cache_lengths,
    norm_gain,
    routes,
    gates,
    gate_proj,
    up_proj,
    down_proj,
):
    new_dev, sequences, q_width = queries.shape
    half = q_width // 2
    half_heads = half // HEAD_SIZE
    z, y, x_lo, x_hi, core = (lax.axis_index(name) for name in ("z", "y", "xl", "xh", "c"))
    z_size, y_size = lax.axis_size("z"), lax.axis_size("y")
    column = z * y_size + y
    columns = z_size * y_size
    ctx_index = column * 2 + x_lo
    ctx_size = 2 * columns
    token_rows = new_dev * sequences

    packed = []
    for cached, new in ((cached_key_rows, new_keys), (cache_values, new_values)):
        packed.append(jnp.concatenate([cached, new], axis=0))
    both = jnp.stack(packed).reshape(2, -1, sequences, 2, HEAD_SIZE)
    low = jnp.transpose(both[:, :, :, 0], (0, 2, 1, 3))
    high = jnp.transpose(both[:, :, :, 1], (0, 2, 1, 3))
    mine = jnp.where(x_lo == 0, low, high)
    theirs = swap(jnp.where(x_lo == 0, high, low), "xl")
    partner_routes = swap(routes, "xl")

    halves = jnp.transpose(queries.reshape(new_dev, sequences, 2, half), (2, 1, 0, 3))
    sent = jnp.broadcast_to(halves[None], (columns, 2, sequences, new_dev, half)).reshape(
        ctx_size, sequences, new_dev, half
    )
    everyone = lax.all_to_all(sent, ("z", "y", "xl"), split_axis=0, concat_axis=0, tiled=True)

    info = jnp.stack(
        [cache_lengths[0], cache_lengths[1], ctx_index, ctx_index ^ 1, column]
    ).astype(jnp.int32)
    partial = attend(info, everyone, mine, theirs)
    got = lax.all_to_all(partial, ("z", "y"), split_axis=0, concat_axis=0, tiled=True)
    attended, square = merge(got)

    square = square[:, :, :1]
    others = [
        lax.ppermute(square, ("xl", "xh", "c"), [(i, i ^ k) for i in range(8)])
        for k in range(1, 8)
    ]
    summed = sum(others, square)
    inverse = lax.rsqrt(summed / (8 * half) + EPS)
    gain = norm_gain.astype(F32)
    own_gain = jnp.where(x_lo == 0, gain[:half], gain[half:])
    normed_half = attended * inverse * own_gain
    payload = normed_half.astype(BF16).reshape(sequences * 2 * new_dev, half)

    split = jnp.transpose(
        normed_half.reshape(sequences, 2, new_dev, half), (1, 2, 0, 3)
    )
    kept = jnp.where(x_lo == 0, split[0], split[1])
    came = swap(jnp.where(x_lo == 0, split[1], split[0]), "xl")
    normed = jnp.concatenate(
        [jnp.where(x_lo == 0, kept, came), jnp.where(x_lo == 0, came, kept)], axis=2
    )

    def slots_of(choice):
        flat = choice.reshape(token_rows * TOPK)
        count = flat.shape[0]
        earlier = jnp.arange(count)[None, :] < jnp.arange(count)[:, None]
        same = flat[:, None] == flat[None, :]
        return flat * CAP + jnp.sum((earlier & same).astype(jnp.int32), axis=1)

    own_target = slots_of(routes)
    partner_target = slots_of(partner_routes)
    targets = jnp.stack(
        [
            jnp.where(x_lo == 0, own_target, partner_target),
            jnp.where(x_lo == 0, partner_target, own_target),
        ]
    ).reshape(2, new_dev, sequences, TOPK)
    targets = jnp.transpose(targets, (2, 0, 1, 3))
    slot_ids = jnp.arange(EXPERTS * CAP).reshape(EXPERTS, 1, CAP, 1, 1, 1, 1)
    of_block = jnp.arange(2).reshape(1, 2, 1, 1, 1, 1, 1)
    block = jnp.arange(2).reshape(1, 1, 1, 1, 2, 1, 1)
    placing = jnp.any(
        (slot_ids == targets[None, None, None]) & (of_block == block), axis=-1
    ).reshape(EXPERTS * 2 * CAP, sequences * 2 * new_dev)
    placed = jnp.dot(placing.astype(BF16), payload, preferred_element_type=F32).astype(BF16)
    group = ctx_size // EXPERTS
    outgoing = jnp.broadcast_to(
        placed.reshape(EXPERTS, 1, 2 * CAP, half), (EXPERTS, 2 * group, 2 * CAP, half)
    ).reshape(2 * ctx_size, 2 * CAP, half)
    near = lax.all_to_all(
        outgoing, ("z", "y", "xl", "xh"), split_axis=0, concat_axis=0, tiled=True
    ).reshape(columns, 4, 2 * CAP, half)
    far = swap(near, "c")

    place = jnp.stack([core, x_hi * 2 + core]).astype(jnp.int32)
    hidden = hidden_units(place, near, far, gate_proj, up_proj)
    hidden_core = swap(hidden, "c")
    hidden_far = swap(hidden, "xh")
    hidden_both = swap(hidden_far, "c")
    produced = block_outputs(place, (hidden, hidden_core, hidden_far, hidden_both), down_proj)
    returned = lax.all_to_all(
        produced.reshape(ctx_size, CAP, q_width),
        ("z", "y", "xl"),
        split_axis=0,
        concat_axis=0,
        tiled=True,
    )

    slot_index = jnp.arange(EXPERTS * CAP).reshape(EXPERTS, 1, CAP, 1, 1)
    weighting = jnp.sum(
        jnp.where(
            slot_index == own_target.reshape(1, 1, 1, token_rows, TOPK),
            gates.reshape(1, 1, 1, token_rows, TOPK),
            0.0,
        ),
        axis=-1,
    )
    weighting = jnp.broadcast_to(weighting, (EXPERTS, group, CAP, token_rows)).reshape(
        ctx_size * CAP, token_rows
    )
    high_part = weighting.astype(BF16)
    rest = weighting - high_part.astype(F32)
    middle_part = rest.astype(BF16)
    low_part = (rest - middle_part.astype(F32)).astype(BF16)
    table = jnp.concatenate([high_part, middle_part, low_part], axis=1)
    mixed = lax.dot_general(
        table,
        returned.reshape(ctx_size * CAP, q_width),
        (((0,), (0,)), ((), ())),
        preferred_element_type=F32,
    ).reshape(3, token_rows, q_width)
    moe_out = (mixed[0] + mixed[1] + mixed[2]).reshape(new_dev, sequences, q_width)
    return (normed, moe_out)


def solution(mesh):
    fine = Mesh(mesh.devices.reshape(4, 4, 2, 2, 2), ("z", "y", "xl", "xh", "c"))
    ctx = ("z", "y", "xl")
    tp = ("xh", "c")
    split = P(ctx, None, tp)
    placed = (
        split,
        split,
        split,
        split,
        split,
        P(),
        P(tp),
        P(ctx, None, None),
        P(ctx, None, None),
        split,
        split,
        split,
    )
    return jax.shard_map(
        on_device,
        mesh=fine,
        in_specs=placed,
        out_specs=(split, split),
        check_vma=False,
    )
```

```python
import math

import jax
import jax.numpy as jnp
from jax import lax
from jax.experimental import pallas as pl
from jax.experimental.pallas import tpu as pltpu
from jax.sharding import Mesh
from jax.sharding import PartitionSpec as P

HEAD_SIZE = 128
EXPERTS = 8
TOPK = 2
CAP = 16
EPS = 1e-05
DEAD = -1e30
LANES = 128
VMEM_LIMIT = 40 * 1024 * 1024

BF16 = jnp.bfloat16
F32 = jnp.float32


def attention_kernel(info_ref, q_ref, *refs, parts, last):
    key_parts, value_parts = refs[:parts], refs[parts : 2 * parts]
    if last:
        before_ref, before_lse_ref, out_ref, keys_ref, values_ref, lse_ref = refs[2 * parts :]
    else:
        out_ref, out_lse_ref, keys_ref, values_ref = refs[2 * parts :]
    sequence = pl.program_id(0)
    group = pl.program_id(1)
    sources, _, own_rows, width = q_ref.shape
    heads = width // HEAD_SIZE
    tokens = sources * own_rows
    count = key_parts[0].shape[0]
    padded = keys_ref.shape[0]
    cache = count - own_rows
    length = info_ref[sequence]
    z_index = info_ref[2]
    lane_index = info_ref[3]
    planes = info_ref[4]
    multiplier = 1.0 / math.sqrt(HEAD_SIZE)
    flag = 4 * own_rows

    for part in range(parts):
        plane = info_ref[5 + part]
        span = slice(part * count, (part + 1) * count)
        keys_ref[span, :LANES] = key_parts[part][...]
        values_ref[span, :LANES] = value_parts[part][...]
        row = lax.broadcasted_iota(jnp.int32, (count, LANES), 0)
        lane = lax.broadcasted_iota(jnp.int32, (count, LANES), 1)
        first = (plane * sources + lane_index) * cache
        dead = (lane == flag) & (row < cache) & (first + row >= length)
        late = (lane - plane * own_rows == row - cache) & (row >= cache)
        keys_ref[span, LANES:] = jnp.where(dead | late, DEAD, 0.0).astype(BF16)
    rest = padded - parts * count
    if rest:
        lane = lax.broadcasted_iota(jnp.int32, (rest, LANES), 1)
        keys_ref[parts * count :, :LANES] = jnp.zeros((rest, LANES), BF16)
        values_ref[parts * count :, :LANES] = jnp.zeros((rest, LANES), BF16)
        keys_ref[parts * count :, LANES:] = jnp.where(lane == flag, DEAD, 0.0).astype(BF16)
    values_ref[:, LANES:] = jnp.ones((padded, LANES), BF16)

    row = lax.broadcasted_iota(jnp.int32, (tokens, LANES), 0)
    lane = lax.broadcasted_iota(jnp.int32, (tokens, LANES), 1)
    position = z_index * tokens + row
    key_position = ((lane // own_rows) * sources + lane_index) * own_rows + lane % own_rows
    blocked = ((lane < planes * own_rows) & (position < key_position)) | (lane == flag)
    causal = jnp.where(blocked, 1.0, 0.0).astype(BF16)

    together = 2
    packed = None
    for start in range(0, heads, together):
        members = range(start, start + together)
        query = jnp.concatenate(
            [
                q_ref[:, 0, :, h * HEAD_SIZE : (h + 1) * HEAD_SIZE].reshape(tokens, HEAD_SIZE)
                for h in members
            ],
            axis=0,
        )
        wide = jnp.concatenate([query, jnp.concatenate([causal] * together, axis=0)], axis=1)
        scores = lax.dot_general(
            wide, keys_ref[...], (((1,), (1,)), ((), ())), preferred_element_type=F32
        )
        top = jnp.max(scores, axis=1, keepdims=True)
        expo = jnp.exp2((scores - top) * (multiplier * math.log2(math.e)))
        mixed = jnp.dot(expo.astype(BF16), values_ref[...], preferred_element_type=F32)
        total = mixed[:, LANES:]
        result = mixed[:, :LANES] / total
        lse = top * multiplier + jnp.log(total)
        rows = slice(start * tokens, (start + together) * tokens)
        if not last:
            out_ref[0, 0, rows] = result
            out_lse_ref[0, 0, rows] = lse
            continue
        other = before_lse_ref[0, 0, rows]
        peak = jnp.maximum(lse, other)
        here, there = jnp.exp(lse - peak), jnp.exp(other - peak)
        both = here + there
        result = (here * result + there * before_ref[0, 0, rows]) / both
        lse = peak + jnp.log(both)
        for place, h in enumerate(members):
            chosen = slice(place * tokens, (place + 1) * tokens)
            out_ref[:, 0, :, pl.ds(group * width + h * HEAD_SIZE, HEAD_SIZE)] = (
                result[chosen].astype(BF16).reshape(sources, own_rows, HEAD_SIZE)
            )
            mark = (lane % 16 == group * heads + h) & (lane < 48)
            packed = jnp.where(mark, lse[chosen], jnp.zeros((tokens, LANES), F32) if packed is None else packed)

    if last:
        @pl.when(group == 0)
        def _():
            lse_ref[...] = packed

        @pl.when(group == pl.num_programs(1) - 1)
        def _():
            value = lse_ref[...] + packed
            high = value.astype(BF16).astype(F32)
            middle = (value - high).astype(BF16).astype(F32)
            low = value - high - middle
            terms = jnp.where(lane < 16, high, jnp.where(lane < 32, middle, low)).astype(BF16)
            edge = out_ref.shape[3] - LANES
            out_ref[:, 0, :, edge:] = terms.reshape(sources, own_rows, LANES)


def attend(info, queries, keys, values, before=None):
    sources, sequences, own_rows, q_width = queries.shape
    parts = len(keys)
    count = keys[0].shape[0]
    groups = keys[0].shape[1] // HEAD_SIZE // sequences
    width = q_width // groups
    padded = -(-parts * count // LANES) * LANES
    rows = sources * own_rows * width // HEAD_SIZE
    key_spec = pl.BlockSpec((count, HEAD_SIZE), lambda s, g, i: (0, s * groups + g))
    state_spec = pl.BlockSpec((1, 1, rows, HEAD_SIZE), lambda s, g, i: (s, g, 0, 0))
    in_specs = [
        pl.BlockSpec((sources, 1, own_rows, width), lambda s, g, i: (0, s, 0, g))
    ] + [key_spec] * (2 * parts)
    scratch = [pltpu.VMEM((padded, 2 * LANES), BF16), pltpu.VMEM((padded, 2 * LANES), BF16)]
    args = [queries, *keys, *values]
    if before is None:
        state = jax.ShapeDtypeStruct((sequences, groups, rows, HEAD_SIZE), F32)
        out_specs, out_shape = [state_spec] * 2, [state] * 2
    else:
        in_specs += [state_spec] * 2
        args += list(before)
        out_specs = pl.BlockSpec(
            (sources, 1, own_rows, q_width + LANES), lambda s, g, i: (0, s, 0, 0)
        )
        out_shape = jax.ShapeDtypeStruct((sources, sequences, own_rows, q_width + LANES), BF16)
        scratch.append(pltpu.VMEM((sources * own_rows, LANES), F32))
    return pl.pallas_call(
        lambda *refs: attention_kernel(*refs, parts=parts, last=before is not None),
        grid_spec=pltpu.PrefetchScalarGridSpec(
            num_scalar_prefetch=1,
            grid=(sequences, groups),
            in_specs=in_specs,
            out_specs=out_specs,
            scratch_shapes=scratch,
        ),
        out_shape=out_shape,
        compiler_params=pltpu.CompilerParams(vmem_limit_bytes=VMEM_LIMIT),
        name="attend",
    )(info, *args)


def merge_kernel(got_ref, placing_ref, gain_ref, out_ref, square_ref, sent_ref):
    sources, sequences, own_rows, wide = got_ref.shape
    rows = sequences * own_rows
    width = wide - LANES
    parts = got_ref[:, :, :, width:].astype(F32).reshape(sources * rows, LANES)
    lse = parts + pltpu.roll(parts, LANES - 16, 1) + pltpu.roll(parts, LANES - 32, 1)
    lse = lse.reshape(sources, rows, LANES)
    weight = jnp.exp(lse - jnp.max(lse, axis=0, keepdims=True))
    weight = weight / jnp.sum(weight, axis=0, keepdims=True)
    pieces = []
    square = jnp.zeros((rows, LANES), F32)
    for head in range(width // HEAD_SIZE):
        lanes = slice(head * HEAD_SIZE, (head + 1) * HEAD_SIZE)
        merged = jnp.zeros((rows, HEAD_SIZE), F32)
        for source in range(sources):
            part = got_ref[source, :, :, lanes].astype(F32).reshape(rows, HEAD_SIZE)
            merged = merged + weight[source, :, head : head + 1] * part
        out_ref[:, :, lanes] = merged.reshape(sequences, own_rows, HEAD_SIZE)
        square = square + merged * merged
        pieces.append((merged * gain_ref[:, lanes]).astype(BF16))
    square = jnp.sum(square, axis=1, keepdims=True)
    square_ref[...] = jnp.broadcast_to(square, (rows, LANES))
    payload = jnp.concatenate(pieces, axis=1)
    placed = jnp.dot(placing_ref[...], payload, preferred_element_type=F32).astype(BF16)
    placed = placed.reshape(EXPERTS, CAP, width)
    copies = sent_ref.shape[0] // EXPERTS
    for expert in range(EXPERTS):
        for copy in range(copies):
            sent_ref[expert * copies + copy] = placed[expert]


def merge(got, placing, gain, targets):
    sources, sequences, own_rows, wide = got.shape
    width = wide - LANES
    return pl.pallas_call(
        merge_kernel,
        out_shape=[
            jax.ShapeDtypeStruct((sequences, own_rows, width), F32),
            jax.ShapeDtypeStruct((sequences * own_rows, LANES), F32),
            jax.ShapeDtypeStruct((targets, CAP, width), BF16),
        ],
        compiler_params=pltpu.CompilerParams(vmem_limit_bytes=VMEM_LIMIT),
        name="merge",
    )(got, placing, gain)


def hidden_kernel(info_ref, *refs, parts):
    rows_refs = refs[: sum(parts)]
    gate_ref, up_ref, scale_ref, out_ref, square_ref = refs[sum(parts) :]
    tile = pl.program_id(0)
    pieces = []
    place = 0
    for index, count in enumerate(parts):
        members = [rows_refs[place + i][...] for i in range(count)]
        place += count
        pieces.append((info_ref[index], members))

    @pl.when(tile == 0)
    def _():
        total = None
        for block, members in pieces:
            rows = jnp.concatenate(members, axis=0) if len(members) > 1 else members[0]
            for start in range(0, rows.shape[1], LANES):
                part = rows[:, start : start + LANES].astype(F32)
                term = part * part * scale_ref[block, :, start : start + LANES]
                total = term if total is None else total + term
        mean = jnp.sum(total, axis=1, keepdims=True) / (len(parts) * rows_refs[0].shape[1])
        square_ref[...] = jnp.broadcast_to(lax.rsqrt(mean + EPS), square_ref.shape)

    gate = up = None
    for block, members in pieces:
        rows = jnp.concatenate(members, axis=0) if len(members) > 1 else members[0]
        gate_term = jnp.dot(rows, gate_ref[block], preferred_element_type=F32)
        up_term = jnp.dot(rows, up_ref[block], preferred_element_type=F32)
        gate = gate_term if gate is None else gate + gate_term
        up = up_term if up is None else up + up_term
    inverse = square_ref[:, :1]
    gate = gate * inverse
    out_ref[...] = (gate / (1.0 + jnp.exp(-gate)) * (up * inverse)).astype(BF16)


def hidden_units(info, pieces, gate_proj, up_proj, scale):
    parts = [len(piece) for piece in pieces]
    rows = [part for piece in pieces for part in piece]
    tokens = sum(part.shape[0] for part in pieces[0])
    width = rows[0].shape[1]
    blocks = len(parts)
    units = gate_proj.shape[2]
    tile = units // 2
    weight = pl.BlockSpec((blocks, width, tile), lambda n, i: (0, 0, n))
    return pl.pallas_call(
        lambda *refs: hidden_kernel(*refs, parts=parts),
        grid_spec=pltpu.PrefetchScalarGridSpec(
            num_scalar_prefetch=1,
            grid=(units // tile,),
            in_specs=[pl.BlockSpec(part.shape, lambda n, i: (0, 0)) for part in rows]
            + [weight, weight, pl.BlockSpec((blocks, 1, width), lambda n, i: (0, 0, 0))],
            out_specs=pl.BlockSpec((tokens, tile), lambda n, i: (0, n)),
            scratch_shapes=[pltpu.VMEM((tokens, LANES), F32)],
        ),
        out_shape=jax.ShapeDtypeStruct((tokens, units), BF16),
        compiler_params=pltpu.CompilerParams(vmem_limit_bytes=VMEM_LIMIT),
        name="hidden_units",
    )(
        info,
        *rows,
        gate_proj.reshape(blocks, width, units),
        up_proj.reshape(blocks, width, units),
        scale,
    )


def down_kernel(info_ref, a_ref, b_ref, c_ref, d_ref, down_ref, *refs):
    mine = info_ref[0]
    units = a_ref.shape[1]
    total = None
    for index, rows_ref in enumerate((a_ref, b_ref, c_ref, d_ref)):
        start = pl.multiple_of((mine ^ index) * units, units)
        term = jnp.dot(
            rows_ref[...], down_ref[0, pl.ds(start, units), :], preferred_element_type=F32
        )
        total = term if total is None else total + term
    if len(refs) > 1:
        total = total + refs[0][...].astype(F32)
    refs[-1][...] = total.astype(BF16)


def block_outputs(info, hiddens, down_proj, added=None):
    tokens, units = hiddens[0].shape
    depth, columns = down_proj.shape[1:]
    tile = 512
    out_spec = pl.BlockSpec((tokens, tile), lambda n, i: (0, n))
    extra = [] if added is None else [added]
    return pl.pallas_call(
        down_kernel,
        grid_spec=pltpu.PrefetchScalarGridSpec(
            num_scalar_prefetch=1,
            grid=(columns // tile,),
            in_specs=[pl.BlockSpec((tokens, units), lambda n, i: (0, 0)) for _ in hiddens]
            + [pl.BlockSpec((1, depth, tile), lambda n, i: (0, 0, n))]
            + [out_spec] * len(extra),
            out_specs=out_spec,
        ),
        out_shape=jax.ShapeDtypeStruct((tokens, columns), BF16),
        compiler_params=pltpu.CompilerParams(vmem_limit_bytes=VMEM_LIMIT),
        name="block_outputs",
    )(info, *hiddens, down_proj, *extra)


def swap(array, axis):
    return lax.ppermute(array, axis, [(0, 1), (1, 0)])


def shift(array, axis, size, by):
    return lax.ppermute(array, axis, [(i, (i + by) % size) for i in range(size)])


def shift_x(array, by):
    index = [(x % 2) * 2 + x // 2 for x in range(4)]
    return lax.ppermute(
        array, ("xl", "xh"), [(index[x], index[(x + by) % 4]) for x in range(4)]
    )


def exchange_hidden(hidden):
    far = swap(hidden, "xh")
    return (hidden, swap(hidden, "c"), far, swap(far, "c"))


def on_device(
    queries,
    new_keys,
    new_values,
    cached_key_rows,
    cache_values,
    cache_lengths,
    norm_gain,
    routes,
    gates,
    gate_proj,
    up_proj,
    down_proj,
):
    new_dev, sequences, q_width = queries.shape
    z, y, x_lo, x_hi, core = (lax.axis_index(name) for name in ("z", "y", "xl", "xh", "c"))
    z_size, y_size = lax.axis_size("z"), lax.axis_size("y")
    columns = z_size * y_size
    token_rows = new_dev * sequences
    group = columns // EXPERTS

    def rows_of(cached, new):
        return jnp.concatenate([cached, new], axis=0).reshape(cached.shape[0] + new_dev, -1)

    own_keys = rows_of(cached_key_rows, new_keys)
    own_values = rows_of(cache_values, new_values)
    keys_up, values_up = shift(own_keys, "z", 4, 1), shift(own_values, "z", 4, 1)
    keys_down, values_down = shift(own_keys, "z", 4, -1), shift(own_values, "z", 4, -1)
    keys_far = shift(keys_up, "z", 4, 1)
    values_far = shift(values_down, "z", 4, -1)

    sent = jnp.broadcast_to(
        jnp.transpose(queries, (1, 0, 2))[None], (2 * y_size, sequences, new_dev, q_width)
    )
    everyone = lax.all_to_all(sent, ("y", "xl"), split_axis=0, concat_axis=0, tiled=True)

    basis = [cache_lengths[0], cache_lengths[1], z, y * 2 + x_lo, jnp.int32(4)]
    near_info = jnp.stack(basis + [z, (z + 3) % 4, (z + 1) % 4]).astype(jnp.int32)
    far_info = jnp.stack(basis + [(z + 2) % 4]).astype(jnp.int32)
    state = attend(
        near_info,
        everyone,
        (own_keys, keys_up, keys_down),
        (own_values, values_up, values_down),
    )
    partial = attend(far_info, everyone, (keys_far,), (values_far,), state)
    got = lax.all_to_all(partial, ("y", "xl"), split_axis=0, concat_axis=0, tiled=True)

    gain = norm_gain.astype(F32)
    gain_core = swap(norm_gain, "c")
    gain_pair = jnp.stack([norm_gain, gain_core])
    gain_pair = jnp.where(core == 0, gain_pair, gain_pair[::-1])
    gain_far = swap(gain_pair, "xh")
    gain_all = jnp.stack([gain_pair, gain_far])
    gain_all = jnp.where(x_hi == 0, gain_all, gain_all[::-1]).astype(F32)
    scales = (1.0 / (gain_all * gain_all)).reshape(4, 1, q_width)

    flat_routes = routes.reshape(token_rows * TOPK)
    order = jnp.arange(token_rows * TOPK)
    earlier = (order[None, :] < order[:, None]) & (flat_routes[:, None] == flat_routes[None, :])
    target = flat_routes * CAP + jnp.sum(earlier.astype(jnp.int32), axis=1)
    by_row = target.reshape(new_dev, sequences, TOPK)
    slot_ids = jnp.arange(EXPERTS * CAP).reshape(EXPERTS * CAP, 1, 1, 1)
    hits = slot_ids == by_row[None]
    placing = jnp.transpose(jnp.any(hits, axis=-1), (0, 2, 1)).reshape(EXPERTS * CAP, token_rows)
    weighting = jnp.sum(jnp.where(hits, gates[None], 0.0), axis=-1).reshape(
        EXPERTS, 1, CAP, token_rows
    )

    attended, square, outgoing = merge(
        got, placing.astype(BF16), gain.reshape(1, q_width), columns
    )
    own_block = lax.all_to_all(
        outgoing, ("z", "y"), split_axis=0, concat_axis=0, tiled=True
    ).reshape(columns * CAP, q_width)

    middle = own_block.shape[0] // 2
    from_below = shift_x(own_block, 1)
    from_above = shift_x(own_block, -1)
    far_low = shift_x(from_below[:middle], 1)
    far_high = shift_x(from_above[middle:], -1)
    own_other = swap(own_block, "c")
    below_other = swap(from_below, "c")
    above_other = swap(from_above, "c")
    far_low_other = swap(far_low, "c")
    far_high_other = swap(far_high, "c")

    below = ((x_hi * 2 + x_lo + 3) % 4) // 2
    above = ((x_hi * 2 + x_lo + 1) % 4) // 2
    first_info = jnp.stack(
        [below * 2 + core, below * 2 + 1 - core, above * 2 + core, above * 2 + 1 - core]
    ).astype(jnp.int32)
    second_info = jnp.stack(
        [
            x_hi * 2 + core,
            x_hi * 2 + 1 - core,
            (1 - x_hi) * 2 + core,
            (1 - x_hi) * 2 + 1 - core,
        ]
    ).astype(jnp.int32)
    place = jnp.reshape(x_hi * 2 + core, (1,)).astype(jnp.int32)
    hidden_first = hidden_units(
        first_info,
        ((from_below,), (below_other,), (from_above,), (above_other,)),
        gate_proj,
        up_proj,
        scales,
    )
    produced_first = block_outputs(place, exchange_hidden(hidden_first), down_proj)
    returned_first = swap(produced_first, "xl")
    hidden_second = hidden_units(
        second_info,
        ((own_block,), (own_other,), (far_low, far_high), (far_low_other, far_high_other)),
        gate_proj,
        up_proj,
        scales,
    )
    produced = block_outputs(
        place, exchange_hidden(hidden_second), down_proj, returned_first
    )

    square = square + swap(square, "c")
    square = square + swap(square, "xh")
    inverse = lax.rsqrt(square[:, :1] / (4 * q_width) + EPS).reshape(sequences, new_dev, 1)
    normed = jnp.transpose(attended * inverse * gain, (1, 0, 2))

    returned = lax.all_to_all(
        produced.reshape(columns, CAP, q_width),
        ("z", "y"),
        split_axis=0,
        concat_axis=0,
        tiled=True,
    )
    weighting = jnp.broadcast_to(weighting, (EXPERTS, group, CAP, token_rows)).reshape(
        columns * CAP, token_rows
    )
    high_part = weighting.astype(BF16)
    rest = weighting - high_part.astype(F32)
    middle_part = rest.astype(BF16)
    low_part = (rest - middle_part.astype(F32)).astype(BF16)
    table = jnp.concatenate([high_part, middle_part, low_part], axis=1)
    mixed = lax.dot_general(
        table,
        returned.reshape(columns * CAP, q_width),
        (((0,), (0,)), ((), ())),
        preferred_element_type=F32,
    ).reshape(3, token_rows, q_width)
    moe_out = (mixed[0] + mixed[1] + mixed[2]).reshape(new_dev, sequences, q_width)
    return (normed, moe_out)


def solution(mesh):
    fine = Mesh(mesh.devices.reshape(4, 4, 2, 2, 2), ("z", "y", "xl", "xh", "c"))
    ctx = ("z", "y", "xl")
    tp = ("xh", "c")
    split = P(ctx, None, tp)
    placed = (
        split,
        split,
        split,
        split,
        split,
        P(),
        P(tp),
        P(ctx, None, None),
        P(ctx, None, None),
        split,
        split,
        split,
    )
    return jax.shard_map(
        on_device,
        mesh=fine,
        in_specs=placed,
        out_specs=(split, split),
        check_vma=False,
    )
```

```python
import math

import jax
import jax.numpy as jnp
from jax import lax
from jax.experimental import pallas as pl
from jax.experimental.pallas import tpu as pltpu
from jax.sharding import Mesh
from jax.sharding import PartitionSpec as P

HEAD_SIZE = 128
EXPERTS = 8
TOPK = 2
CAP = 16
EPS = 1e-05
DEAD = -1e30
LANES = 128
VMEM_LIMIT = 20 * 1024 * 1024
SMALL_LIMIT = 10 * 1024 * 1024

BF16 = jnp.bfloat16
F32 = jnp.float32


def attention_kernel(info_ref, q_ref, *refs, parts, last):
    key_parts, value_parts = refs[:parts], refs[parts : 2 * parts]
    if last:
        before_ref, before_lse_ref, out_ref, keys_ref, values_ref, lse_ref = refs[2 * parts :]
    else:
        out_ref, out_lse_ref, keys_ref, values_ref = refs[2 * parts :]
    sequence = pl.program_id(0)
    group = pl.program_id(1)
    sources, _, own_rows, width = q_ref.shape
    heads = width // HEAD_SIZE
    tokens = sources * own_rows
    count = key_parts[0].shape[0]
    padded = keys_ref.shape[0]
    cache = count - own_rows
    length = info_ref[sequence]
    z_index = info_ref[2]
    lane_index = info_ref[3]
    planes = info_ref[4]
    multiplier = 1.0 / math.sqrt(HEAD_SIZE)
    flag = 4 * own_rows

    for part in range(parts):
        plane = info_ref[5 + part]
        span = slice(part * count, (part + 1) * count)
        keys_ref[span, :LANES] = key_parts[part][...]
        values_ref[span, :LANES] = value_parts[part][...]
        row = lax.broadcasted_iota(jnp.int32, (count, LANES), 0)
        lane = lax.broadcasted_iota(jnp.int32, (count, LANES), 1)
        first = (plane * sources + lane_index) * cache
        dead = (lane == flag) & (row < cache) & (first + row >= length)
        late = (lane - plane * own_rows == row - cache) & (row >= cache)
        keys_ref[span, LANES:] = jnp.where(dead | late, DEAD, 0.0).astype(BF16)
    rest = padded - parts * count
    if rest:
        lane = lax.broadcasted_iota(jnp.int32, (rest, LANES), 1)
        keys_ref[parts * count :, :LANES] = jnp.zeros((rest, LANES), BF16)
        values_ref[parts * count :, :LANES] = jnp.zeros((rest, LANES), BF16)
        keys_ref[parts * count :, LANES:] = jnp.where(lane == flag, DEAD, 0.0).astype(BF16)
    values_ref[:, LANES:] = jnp.ones((padded, LANES), BF16)

    row = lax.broadcasted_iota(jnp.int32, (tokens, LANES), 0)
    lane = lax.broadcasted_iota(jnp.int32, (tokens, LANES), 1)
    position = z_index * tokens + row
    key_position = ((lane // own_rows) * sources + lane_index) * own_rows + lane % own_rows
    blocked = ((lane < planes * own_rows) & (position < key_position)) | (lane == flag)
    causal = jnp.where(blocked, 1.0, 0.0).astype(BF16)

    together = 2
    packed = None
    for start in range(0, heads, together):
        members = range(start, start + together)
        query = jnp.concatenate(
            [
                q_ref[:, 0, :, h * HEAD_SIZE : (h + 1) * HEAD_SIZE].reshape(tokens, HEAD_SIZE)
                for h in members
            ],
            axis=0,
        )
        wide = jnp.concatenate([query, jnp.concatenate([causal] * together, axis=0)], axis=1)
        scores = lax.dot_general(
            wide, keys_ref[...], (((1,), (1,)), ((), ())), preferred_element_type=F32
        )
        top = jnp.max(scores, axis=1, keepdims=True)
        expo = jnp.exp2((scores - top) * (multiplier * math.log2(math.e)))
        mixed = jnp.dot(expo.astype(BF16), values_ref[...], preferred_element_type=F32)
        total = mixed[:, LANES:]
        result = mixed[:, :LANES] / total
        lse = top * multiplier + jnp.log(total)
        rows = slice(start * tokens, (start + together) * tokens)
        if not last:
            out_ref[0, 0, rows] = result
            out_lse_ref[0, 0, rows] = lse
            continue
        other = before_lse_ref[0, 0, rows]
        peak = jnp.maximum(lse, other)
        here, there = jnp.exp(lse - peak), jnp.exp(other - peak)
        both = here + there
        result = (here * result + there * before_ref[0, 0, rows]) / both
        lse = peak + jnp.log(both)
        for place, h in enumerate(members):
            chosen = slice(place * tokens, (place + 1) * tokens)
            out_ref[:, 0, :, pl.ds(group * width + h * HEAD_SIZE, HEAD_SIZE)] = (
                result[chosen].astype(BF16).reshape(sources, own_rows, HEAD_SIZE)
            )
            mark = (lane % 16 == group * heads + h) & (lane < 48)
            packed = jnp.where(mark, lse[chosen], jnp.zeros((tokens, LANES), F32) if packed is None else packed)

    if last:
        @pl.when(group == 0)
        def _():
            lse_ref[...] = packed

        @pl.when(group == pl.num_programs(1) - 1)
        def _():
            value = lse_ref[...] + packed
            high = value.astype(BF16).astype(F32)
            middle = (value - high).astype(BF16).astype(F32)
            low = value - high - middle
            terms = jnp.where(lane < 16, high, jnp.where(lane < 32, middle, low)).astype(BF16)
            edge = out_ref.shape[3] - LANES
            out_ref[:, 0, :, edge:] = terms.reshape(sources, own_rows, LANES)


def attend(info, queries, keys, values, before=None):
    sources, sequences, own_rows, q_width = queries.shape
    parts = len(keys)
    count = keys[0].shape[0]
    groups = keys[0].shape[1] // HEAD_SIZE // sequences
    width = q_width // groups
    padded = -(-parts * count // LANES) * LANES
    rows = sources * own_rows * width // HEAD_SIZE
    key_spec = pl.BlockSpec((count, HEAD_SIZE), lambda s, g, i: (0, s * groups + g))
    state_spec = pl.BlockSpec((1, 1, rows, HEAD_SIZE), lambda s, g, i: (s, g, 0, 0))
    in_specs = [
        pl.BlockSpec((sources, 1, own_rows, width), lambda s, g, i: (0, s, 0, g))
    ] + [key_spec] * (2 * parts)
    scratch = [pltpu.VMEM((padded, 2 * LANES), BF16), pltpu.VMEM((padded, 2 * LANES), BF16)]
    args = [queries, *keys, *values]
    if before is None:
        state = jax.ShapeDtypeStruct((sequences, groups, rows, HEAD_SIZE), F32)
        out_specs, out_shape = [state_spec] * 2, [state] * 2
    else:
        in_specs += [state_spec] * 2
        args += list(before)
        out_specs = pl.BlockSpec(
            (sources, 1, own_rows, q_width + LANES), lambda s, g, i: (0, s, 0, 0)
        )
        out_shape = jax.ShapeDtypeStruct((sources, sequences, own_rows, q_width + LANES), BF16)
        scratch.append(pltpu.VMEM((sources * own_rows, LANES), F32))
    return pl.pallas_call(
        lambda *refs: attention_kernel(*refs, parts=parts, last=before is not None),
        grid_spec=pltpu.PrefetchScalarGridSpec(
            num_scalar_prefetch=1,
            grid=(sequences, groups),
            in_specs=in_specs,
            out_specs=out_specs,
            scratch_shapes=scratch,
        ),
        out_shape=out_shape,
        compiler_params=pltpu.CompilerParams(vmem_limit_bytes=VMEM_LIMIT),
        cost_estimate=cost(
            8 * sequences * groups * rows * padded * HEAD_SIZE,
            args,
            sequences * groups * rows * padded,
        ),
        name="attend",
    )(info, *args)


def merge_kernel(got_ref, placing_ref, gain_ref, out_ref, square_ref, sent_ref):
    sources, sequences, own_rows, wide = got_ref.shape
    rows = sequences * own_rows
    width = wide - LANES
    parts = got_ref[:, :, :, width:].astype(F32).reshape(sources * rows, LANES)
    lse = parts + pltpu.roll(parts, LANES - 16, 1) + pltpu.roll(parts, LANES - 32, 1)
    lse = lse.reshape(sources, rows, LANES)
    weight = jnp.exp(lse - jnp.max(lse, axis=0, keepdims=True))
    weight = weight / jnp.sum(weight, axis=0, keepdims=True)
    pieces = []
    square = jnp.zeros((rows, LANES), F32)
    for head in range(width // HEAD_SIZE):
        lanes = slice(head * HEAD_SIZE, (head + 1) * HEAD_SIZE)
        merged = jnp.zeros((rows, HEAD_SIZE), F32)
        for source in range(sources):
            part = got_ref[source, :, :, lanes].astype(F32).reshape(rows, HEAD_SIZE)
            merged = merged + weight[source, :, head : head + 1] * part
        out_ref[:, :, lanes] = merged.reshape(sequences, own_rows, HEAD_SIZE)
        square = square + merged * merged
        pieces.append((merged * gain_ref[:, lanes]).astype(BF16))
    square = jnp.sum(square, axis=1, keepdims=True)
    square_ref[...] = jnp.broadcast_to(square, (rows, LANES))
    payload = jnp.concatenate(pieces, axis=1)
    placed = jnp.dot(placing_ref[...], payload, preferred_element_type=F32).astype(BF16)
    placed = placed.reshape(EXPERTS, CAP, width)
    copies = sent_ref.shape[0] // EXPERTS
    for expert in range(EXPERTS):
        for copy in range(copies):
            sent_ref[expert * copies + copy] = placed[expert]


def merge(got, placing, gain, targets):
    sources, sequences, own_rows, wide = got.shape
    width = wide - LANES
    return pl.pallas_call(
        merge_kernel,
        out_shape=[
            jax.ShapeDtypeStruct((sequences, own_rows, width), F32),
            jax.ShapeDtypeStruct((sequences * own_rows, LANES), F32),
            jax.ShapeDtypeStruct((targets, CAP, width), BF16),
        ],
        compiler_params=pltpu.CompilerParams(vmem_limit_bytes=VMEM_LIMIT),
        cost_estimate=cost(8 * got.size, [got, got]),
        name="merge",
    )(got, placing, gain)


def hidden_kernel(info_ref, *refs, parts):
    rows_refs = refs[: sum(parts)]
    gate_ref, up_ref, scale_ref, out_ref = refs[sum(parts) :]
    units = out_ref.shape[1]
    width = rows_refs[0].shape[1]
    pieces = []
    place = 0
    for index, count in enumerate(parts):
        members = [rows_refs[place + i][...] for i in range(count)]
        place += count
        rows = jnp.concatenate(members, axis=0) if count > 1 else members[0]
        pieces.append((info_ref[index], rows))
    total = None
    for block, rows in pieces:
        for start in range(0, width, LANES):
            part = rows[:, start : start + LANES].astype(F32)
            term = part * part * scale_ref[block, :, start : start + LANES]
            total = term if total is None else total + term
    mean = jnp.sum(total, axis=1, keepdims=True) / (len(parts) * width)
    inverse = lax.rsqrt(mean + EPS)
    tile = units // 2
    for lane in range(0, units, tile):
        gate = up = None
        for block, rows in pieces:
            span = pl.ds(pl.multiple_of(block * width, LANES), width)
            gate_term = jnp.dot(
                rows, gate_ref[span, lane : lane + tile], preferred_element_type=F32
            )
            up_term = jnp.dot(rows, up_ref[span, lane : lane + tile], preferred_element_type=F32)
            gate = gate_term if gate is None else gate + gate_term
            up = up_term if up is None else up + up_term
        gate = gate * inverse
        out_ref[:, lane : lane + tile] = (
            gate / (1.0 + jnp.exp(-gate)) * (up * inverse)
        ).astype(BF16)


def hidden_units(info, pieces, w_gate, w_up, scale):
    parts = [len(piece) for piece in pieces]
    rows = [part for piece in pieces for part in piece]
    tokens = sum(part.shape[0] for part in pieces[0])
    return pl.pallas_call(
        lambda *refs: hidden_kernel(*refs, parts=parts),
        in_specs=[pl.BlockSpec(memory_space=pltpu.SMEM)]
        + [pl.BlockSpec(memory_space=pltpu.VMEM)] * (len(rows) + 3),
        out_shape=jax.ShapeDtypeStruct((tokens, w_gate.shape[1]), BF16),
        compiler_params=pltpu.CompilerParams(vmem_limit_bytes=SMALL_LIMIT),
        cost_estimate=cost(4 * tokens * w_gate.size, [*rows, w_gate, w_up]),
        name="hidden_units",
    )(info, *rows, w_gate, w_up, scale)


def down_kernel(info_ref, a_ref, b_ref, c_ref, d_ref, down_ref, *refs):
    mine = info_ref[0]
    units = a_ref.shape[1]
    tile = 512
    for lane in range(0, down_ref.shape[1], tile):
        total = None
        for index, rows_ref in enumerate((a_ref, b_ref, c_ref, d_ref)):
            start = pl.multiple_of((mine ^ index) * units, units)
            term = jnp.dot(
                rows_ref[...],
                down_ref[pl.ds(start, units), lane : lane + tile],
                preferred_element_type=F32,
            )
            total = term if total is None else total + term
        result = total.astype(BF16)
        if len(refs) == 1:
            refs[0][:, lane : lane + tile] = result
            continue
        before_ref, out_ref = refs
        sources, _, count, _ = out_ref.shape
        here, there = pl.ds(info_ref[1], 1), pl.ds(1 - info_ref[1], 1)
        out_ref[:, here, :, lane : lane + tile] = result.reshape(sources, 1, count, tile)
        out_ref[:, there, :, lane : lane + tile] = before_ref[:, lane : lane + tile].reshape(
            sources, 1, count, tile
        )


def block_outputs(info, hiddens, w_down, before=None):
    tokens = hiddens[0].shape[0]
    columns = w_down.shape[1]
    args = [*hiddens, w_down]
    out_shape = (tokens, columns)
    if before is not None:
        args.append(before)
        out_shape = (tokens // CAP, 2, CAP, columns)
    return pl.pallas_call(
        down_kernel,
        in_specs=[pl.BlockSpec(memory_space=pltpu.SMEM)]
        + [pl.BlockSpec(memory_space=pltpu.VMEM)] * len(args),
        out_shape=jax.ShapeDtypeStruct(out_shape, BF16),
        compiler_params=pltpu.CompilerParams(vmem_limit_bytes=SMALL_LIMIT),
        cost_estimate=cost(2 * tokens * w_down.size, [w_down, w_down]),
        name="block_outputs",
    )(info, *args)


def cost(flops, arrays, transcendentals=0):
    size = sum(array.size * array.dtype.itemsize for array in arrays)
    return pl.CostEstimate(
        flops=flops, bytes_accessed=size, transcendentals=transcendentals
    )


def swap(array, axis):
    return lax.ppermute(array, axis, [(0, 1), (1, 0)])


def shift(array, axis, size, by):
    return lax.ppermute(array, axis, [(i, (i + by) % size) for i in range(size)])


def shift_x(array, by):
    index = [(x % 2) * 2 + x // 2 for x in range(4)]
    return lax.ppermute(
        array, ("xl", "xh"), [(index[x], index[(x + by) % 4]) for x in range(4)]
    )


def on_device(
    queries,
    new_keys,
    new_values,
    cached_key_rows,
    cache_values,
    cache_lengths,
    norm_gain,
    routes,
    gates,
    gate_proj,
    up_proj,
    down_proj,
):
    new_dev, sequences, q_width = queries.shape
    z, y, x_lo, x_hi, core = (lax.axis_index(name) for name in ("z", "y", "xl", "xh", "c"))
    z_size, y_size = lax.axis_size("z"), lax.axis_size("y")
    columns = z_size * y_size
    token_rows = new_dev * sequences
    group = columns // EXPERTS

    def rows_of(cached, new):
        return jnp.concatenate([cached, new], axis=0).reshape(cached.shape[0] + new_dev, -1)

    own_keys = rows_of(cached_key_rows, new_keys)
    own_values = rows_of(cache_values, new_values)
    keys_up, values_up = shift(own_keys, "z", 4, 1), shift(own_values, "z", 4, 1)
    keys_down, values_down = shift(own_keys, "z", 4, -1), shift(own_values, "z", 4, -1)
    keys_far = shift(keys_up, "z", 4, 1)
    values_far = shift(values_down, "z", 4, -1)

    sent = jnp.broadcast_to(
        jnp.transpose(queries, (1, 0, 2))[None], (2 * y_size, sequences, new_dev, q_width)
    )
    everyone = lax.all_to_all(sent, ("y", "xl"), split_axis=0, concat_axis=0, tiled=True)

    basis = [cache_lengths[0], cache_lengths[1], z, y * 2 + x_lo, jnp.int32(4)]
    near_info = jnp.stack(basis + [z, (z + 3) % 4, (z + 1) % 4]).astype(jnp.int32)
    far_info = jnp.stack(basis + [(z + 2) % 4]).astype(jnp.int32)
    state = attend(
        near_info,
        everyone,
        (own_keys, keys_up, keys_down),
        (own_values, values_up, values_down),
    )
    partial = attend(far_info, everyone, (keys_far,), (values_far,), state)
    got = lax.all_to_all(partial, ("y", "xl"), split_axis=0, concat_axis=0, tiled=True)

    gain = norm_gain.astype(F32)
    gain_core = swap(norm_gain, "c")
    gain_pair = jnp.where(
        core == 0, jnp.stack([norm_gain, gain_core]), jnp.stack([gain_core, norm_gain])
    )
    gain_far = swap(gain_pair, "xh")
    gain_all = jnp.where(
        x_hi == 0, jnp.stack([gain_pair, gain_far]), jnp.stack([gain_far, gain_pair])
    ).astype(F32)
    scales = (1.0 / (gain_all * gain_all)).reshape(4, 1, q_width)

    flat_routes = routes.reshape(token_rows * TOPK)
    order = jnp.arange(token_rows * TOPK)
    earlier = (order[None, :] < order[:, None]) & (flat_routes[:, None] == flat_routes[None, :])
    target = flat_routes * CAP + jnp.sum(earlier.astype(jnp.int32), axis=1)
    by_row = target.reshape(new_dev, sequences, TOPK)
    slot_ids = jnp.arange(EXPERTS * CAP).reshape(EXPERTS * CAP, 1, 1, 1)
    hits = slot_ids == by_row[None]
    placing = jnp.transpose(jnp.any(hits, axis=-1), (0, 2, 1)).reshape(EXPERTS * CAP, token_rows)
    weighting = jnp.sum(jnp.where(hits, gates[None], 0.0), axis=-1).reshape(
        EXPERTS, 1, CAP, token_rows
    )

    attended, square, outgoing = merge(
        got, placing.astype(BF16), gain.reshape(1, q_width), columns
    )
    outgoing, scales = lax.optimization_barrier((outgoing, scales))
    own_block = lax.all_to_all(
        outgoing, ("z", "y"), split_axis=0, concat_axis=0, tiled=True
    ).reshape(columns * CAP, q_width)
    w_gate, w_up, w_down = gate_proj[0], up_proj[0], down_proj[0]

    middle = own_block.shape[0] // 2
    from_below = shift_x(own_block, 1)
    from_above = shift_x(own_block, -1)
    far_low = shift_x(from_below[:middle], 1)
    far_high = shift_x(from_above[middle:], -1)
    own_other = swap(own_block, "c")
    below_other = swap(from_below, "c")
    above_other = swap(from_above, "c")

    below = ((x_hi * 2 + x_lo + 3) % 4) // 2
    above = ((x_hi * 2 + x_lo + 1) % 4) // 2
    first_info = jnp.stack(
        [below * 2 + core, below * 2 + 1 - core, above * 2 + core, above * 2 + 1 - core]
    ).astype(jnp.int32)
    second_info = jnp.stack(
        [
            x_hi * 2 + core,
            x_hi * 2 + 1 - core,
            (1 - x_hi) * 2 + core,
            (1 - x_hi) * 2 + 1 - core,
        ]
    ).astype(jnp.int32)
    place = jnp.stack([x_hi * 2 + core, x_lo]).astype(jnp.int32)
    hidden_first = hidden_units(
        first_info,
        ((from_below,), (below_other,), (from_above,), (above_other,)),
        w_gate,
        w_up,
        scales,
    )
    far_low, far_high, hidden_first = lax.optimization_barrier((far_low, far_high, hidden_first))
    first_far, first_other = swap(hidden_first, "xh"), swap(hidden_first, "c")
    hidden_second = hidden_units(
        second_info,
        (
            (own_block,),
            (own_other,),
            (far_low, far_high),
            (swap(far_low, "c"), swap(far_high, "c")),
        ),
        w_gate,
        w_up,
        scales,
    )
    first_far, hidden_second = lax.optimization_barrier((first_far, hidden_second))
    second_far, second_other = swap(hidden_second, "xh"), swap(hidden_second, "c")
    produced_first = block_outputs(
        place, (hidden_first, first_other, first_far, swap(first_far, "c")), w_down
    )
    second_far, produced_first = lax.optimization_barrier((second_far, produced_first))
    produced = block_outputs(
        place,
        (hidden_second, second_other, second_far, swap(second_far, "c")),
        w_down,
        produced_first,
    )

    square = square + swap(square, "c")
    square = square + swap(square, "xh")
    inverse = lax.rsqrt(square[:, :1] / (4 * q_width) + EPS).reshape(sequences, new_dev, 1)
    normed = jnp.transpose(attended * inverse * gain, (1, 0, 2))

    rows_back = 2 * columns * CAP
    returned = lax.all_to_all(
        produced.reshape(2 * columns, CAP, q_width),
        ("z", "y", "xl"),
        split_axis=0,
        concat_axis=0,
        tiled=True,
    )
    weighting = jnp.broadcast_to(weighting, (EXPERTS, 2 * group, CAP, token_rows)).reshape(
        rows_back, token_rows
    )
    high_part = weighting.astype(BF16)
    rest = weighting - high_part.astype(F32)
    middle_part = rest.astype(BF16)
    low_part = (rest - middle_part.astype(F32)).astype(BF16)
    table = jnp.concatenate([high_part, middle_part, low_part], axis=1)
    mixed = lax.dot_general(
        table,
        returned.reshape(rows_back, q_width),
        (((0,), (0,)), ((), ())),
        preferred_element_type=F32,
    ).reshape(3, token_rows, q_width)
    moe_out = (mixed[0] + mixed[1] + mixed[2]).reshape(new_dev, sequences, q_width)
    return (normed, moe_out)


def solution(mesh):
    fine = Mesh(mesh.devices.reshape(4, 4, 2, 2, 2), ("z", "y", "xl", "xh", "c"))
    ctx = ("z", "y", "xl")
    tp = ("xh", "c")
    split = P(ctx, None, tp)
    placed = (
        split,
        split,
        split,
        split,
        split,
        P(),
        P(tp),
        P(ctx, None, None),
        P(ctx, None, None),
        split,
        split,
        split,
    )
    return jax.shard_map(
        on_device,
        mesh=fine,
        in_specs=placed,
        out_specs=(split, split),
        check_vma=False,
    )
```

```python
import math

import jax
import jax.numpy as jnp
from jax import lax
from jax.experimental import pallas as pl
from jax.experimental.pallas import tpu as pltpu
from jax.sharding import Mesh
from jax.sharding import PartitionSpec as P

HEAD_SIZE = 128
EXPERTS = 8
TOPK = 2
CAP = 16
EPS = 1e-05
DEAD = -1e30
LANES = 128
VMEM_LIMIT = 20 * 1024 * 1024
SMALL_LIMIT = 10 * 1024 * 1024

BF16 = jnp.bfloat16
F32 = jnp.float32


def attention_kernel(info_ref, q_ref, *refs, parts, last):
    key_parts, value_parts = refs[:parts], refs[parts : 2 * parts]
    if last:
        before_ref, before_lse_ref, out_ref, keys_ref, values_ref, lse_ref = refs[2 * parts :]
    else:
        out_ref, out_lse_ref, keys_ref, values_ref = refs[2 * parts :]
    sequence = pl.program_id(0)
    group = pl.program_id(1)
    sources, _, own_rows, width = q_ref.shape
    heads = width // HEAD_SIZE
    tokens = sources * own_rows
    count = key_parts[0].shape[0]
    padded = keys_ref.shape[0]
    cache = count - own_rows
    length = info_ref[sequence]
    z_index = info_ref[2]
    lane_index = info_ref[3]
    planes = info_ref[4]
    multiplier = 1.0 / math.sqrt(HEAD_SIZE)
    flag = 4 * own_rows

    for part in range(parts):
        plane = info_ref[5 + part]
        span = slice(part * count, (part + 1) * count)
        keys_ref[span, :LANES] = key_parts[part][...]
        values_ref[span, :LANES] = value_parts[part][...]
        row = lax.broadcasted_iota(jnp.int32, (count, LANES), 0)
        lane = lax.broadcasted_iota(jnp.int32, (count, LANES), 1)
        first = (plane * sources + lane_index) * cache
        dead = (lane == flag) & (row < cache) & (first + row >= length)
        late = (lane - plane * own_rows == row - cache) & (row >= cache)
        keys_ref[span, LANES:] = jnp.where(dead | late, DEAD, 0.0).astype(BF16)
    rest = padded - parts * count
    if rest:
        lane = lax.broadcasted_iota(jnp.int32, (rest, LANES), 1)
        keys_ref[parts * count :, :LANES] = jnp.zeros((rest, LANES), BF16)
        values_ref[parts * count :, :LANES] = jnp.zeros((rest, LANES), BF16)
        keys_ref[parts * count :, LANES:] = jnp.where(lane == flag, DEAD, 0.0).astype(BF16)
    values_ref[:, LANES:] = jnp.ones((padded, LANES), BF16)

    row = lax.broadcasted_iota(jnp.int32, (tokens, LANES), 0)
    lane = lax.broadcasted_iota(jnp.int32, (tokens, LANES), 1)
    position = z_index * tokens + row
    key_position = ((lane // own_rows) * sources + lane_index) * own_rows + lane % own_rows
    blocked = ((lane < planes * own_rows) & (position < key_position)) | (lane == flag)
    causal = jnp.where(blocked, 1.0, 0.0).astype(BF16)

    together = 2
    packed = None
    for start in range(0, heads, together):
        members = range(start, start + together)
        query = jnp.concatenate(
            [
                q_ref[:, 0, :, h * HEAD_SIZE : (h + 1) * HEAD_SIZE].reshape(tokens, HEAD_SIZE)
                for h in members
            ],
            axis=0,
        )
        wide = jnp.concatenate([query, jnp.concatenate([causal] * together, axis=0)], axis=1)
        scores = lax.dot_general(
            wide, keys_ref[...], (((1,), (1,)), ((), ())), preferred_element_type=F32
        )
        top = jnp.max(scores, axis=1, keepdims=True)
        expo = jnp.exp2((scores - top) * (multiplier * math.log2(math.e)))
        mixed = jnp.dot(expo.astype(BF16), values_ref[...], preferred_element_type=F32)
        total = mixed[:, LANES:]
        result = mixed[:, :LANES] / total
        lse = top * multiplier + jnp.log(total)
        rows = slice(start * tokens, (start + together) * tokens)
        if not last:
            out_ref[0, 0, rows] = result
            out_lse_ref[0, 0, rows] = lse
            continue
        other = before_lse_ref[0, 0, rows]
        peak = jnp.maximum(lse, other)
        here, there = jnp.exp(lse - peak), jnp.exp(other - peak)
        both = here + there
        result = (here * result + there * before_ref[0, 0, rows]) / both
        lse = peak + jnp.log(both)
        for place, h in enumerate(members):
            chosen = slice(place * tokens, (place + 1) * tokens)
            out_ref[:, 0, :, pl.ds(group * width + h * HEAD_SIZE, HEAD_SIZE)] = (
                result[chosen].astype(BF16).reshape(sources, own_rows, HEAD_SIZE)
            )
            mark = (lane % 16 == group * heads + h) & (lane < 48)
            packed = jnp.where(mark, lse[chosen], jnp.zeros((tokens, LANES), F32) if packed is None else packed)

    if last:
        @pl.when(group == 0)
        def _():
            lse_ref[...] = packed

        @pl.when(group == pl.num_programs(1) - 1)
        def _():
            value = lse_ref[...] + packed
            high = value.astype(BF16).astype(F32)
            middle = (value - high).astype(BF16).astype(F32)
            low = value - high - middle
            terms = jnp.where(lane < 16, high, jnp.where(lane < 32, middle, low)).astype(BF16)
            edge = out_ref.shape[3] - LANES
            out_ref[:, 0, :, edge:] = terms.reshape(sources, own_rows, LANES)


def attend(info, queries, keys, values, before=None):
    sources, sequences, own_rows, q_width = queries.shape
    parts = len(keys)
    count = keys[0].shape[0]
    groups = keys[0].shape[1] // HEAD_SIZE // sequences
    width = q_width // groups
    padded = -(-parts * count // LANES) * LANES
    rows = sources * own_rows * width // HEAD_SIZE
    key_spec = pl.BlockSpec((count, HEAD_SIZE), lambda s, g, i: (0, s * groups + g))
    state_spec = pl.BlockSpec((1, 1, rows, HEAD_SIZE), lambda s, g, i: (s, g, 0, 0))
    in_specs = [
        pl.BlockSpec((sources, 1, own_rows, width), lambda s, g, i: (0, s, 0, g))
    ] + [key_spec] * (2 * parts)
    scratch = [pltpu.VMEM((padded, 2 * LANES), BF16), pltpu.VMEM((padded, 2 * LANES), BF16)]
    args = [queries, *keys, *values]
    if before is None:
        state = jax.ShapeDtypeStruct((sequences, groups, rows, HEAD_SIZE), F32)
        out_specs, out_shape = [state_spec] * 2, [state] * 2
    else:
        in_specs += [state_spec] * 2
        args += list(before)
        out_specs = pl.BlockSpec(
            (sources, 1, own_rows, q_width + LANES), lambda s, g, i: (0, s, 0, 0)
        )
        out_shape = jax.ShapeDtypeStruct((sources, sequences, own_rows, q_width + LANES), BF16)
        scratch.append(pltpu.VMEM((sources * own_rows, LANES), F32))
    return pl.pallas_call(
        lambda *refs: attention_kernel(*refs, parts=parts, last=before is not None),
        grid_spec=pltpu.PrefetchScalarGridSpec(
            num_scalar_prefetch=1,
            grid=(sequences, groups),
            in_specs=in_specs,
            out_specs=out_specs,
            scratch_shapes=scratch,
        ),
        out_shape=out_shape,
        compiler_params=pltpu.CompilerParams(vmem_limit_bytes=VMEM_LIMIT),
        cost_estimate=cost(
            8 * sequences * groups * rows * padded * HEAD_SIZE,
            args,
            sequences * groups * rows * padded,
        ),
        name="attend",
    )(info, *args)


def merge_kernel(got_ref, placing_ref, gain_ref, out_ref, square_ref, sent_ref):
    sources, sequences, own_rows, wide = got_ref.shape
    rows = sequences * own_rows
    width = wide - LANES
    parts = got_ref[:, :, :, width:].astype(F32).reshape(sources * rows, LANES)
    lse = parts + pltpu.roll(parts, LANES - 16, 1) + pltpu.roll(parts, LANES - 32, 1)
    lse = lse.reshape(sources, rows, LANES)
    weight = jnp.exp(lse - jnp.max(lse, axis=0, keepdims=True))
    weight = weight / jnp.sum(weight, axis=0, keepdims=True)
    pieces = []
    square = jnp.zeros((rows, LANES), F32)
    for head in range(width // HEAD_SIZE):
        lanes = slice(head * HEAD_SIZE, (head + 1) * HEAD_SIZE)
        merged = jnp.zeros((rows, HEAD_SIZE), F32)
        for source in range(sources):
            part = got_ref[source, :, :, lanes].astype(F32).reshape(rows, HEAD_SIZE)
            merged = merged + weight[source, :, head : head + 1] * part
        out_ref[:, :, lanes] = merged.reshape(sequences, own_rows, HEAD_SIZE)
        square = square + merged * merged
        pieces.append((merged * gain_ref[:, lanes]).astype(BF16))
    square = jnp.sum(square, axis=1, keepdims=True)
    square_ref[...] = jnp.broadcast_to(square, (rows, LANES))
    payload = jnp.concatenate(pieces, axis=1)
    placed = jnp.dot(placing_ref[...], payload, preferred_element_type=F32).astype(BF16)
    placed = placed.reshape(EXPERTS, CAP, width)
    copies = sent_ref.shape[0] // EXPERTS
    for expert in range(EXPERTS):
        for copy in range(copies):
            sent_ref[expert * copies + copy] = placed[expert]


def merge(got, placing, gain, targets):
    sources, sequences, own_rows, wide = got.shape
    width = wide - LANES
    return pl.pallas_call(
        merge_kernel,
        out_shape=[
            jax.ShapeDtypeStruct((sequences, own_rows, width), F32),
            jax.ShapeDtypeStruct((sequences * own_rows, LANES), F32),
            jax.ShapeDtypeStruct((targets, CAP, width), BF16),
        ],
        compiler_params=pltpu.CompilerParams(vmem_limit_bytes=VMEM_LIMIT),
        cost_estimate=cost(8 * got.size, [got, got]),
        name="merge",
    )(got, placing, gain)


def halves_kernel(below_ref, above_ref, low_ref, high_ref):
    middle = low_ref.shape[0]
    low_ref[...] = below_ref[:middle]
    high_ref[...] = above_ref[middle:]


def halves(below, above):
    rows, width = below.shape
    half = jax.ShapeDtypeStruct((rows // 2, width), BF16)
    return pl.pallas_call(
        halves_kernel,
        in_specs=[pl.BlockSpec(memory_space=pltpu.VMEM)] * 2,
        out_specs=[pl.BlockSpec(memory_space=pltpu.VMEM)] * 2,
        out_shape=[half, half],
        compiler_params=pltpu.CompilerParams(vmem_limit_bytes=SMALL_LIMIT),
        cost_estimate=cost(0, [below, above]),
        name="halves",
    )(below, above)


def hidden_kernel(info_ref, *refs, parts):
    rows_refs = refs[: sum(parts)]
    gate_ref, up_ref, scale_ref, out_ref = refs[sum(parts) :]
    units = out_ref.shape[1]
    width = rows_refs[0].shape[1]
    pieces = []
    place = 0
    for index, count in enumerate(parts):
        members = [rows_refs[place + i][...] for i in range(count)]
        place += count
        rows = jnp.concatenate(members, axis=0) if count > 1 else members[0]
        pieces.append((info_ref[index], rows))
    total = None
    for block, rows in pieces:
        for start in range(0, width, LANES):
            part = rows[:, start : start + LANES].astype(F32)
            term = part * part * scale_ref[block, :, start : start + LANES]
            total = term if total is None else total + term
    mean = jnp.sum(total, axis=1, keepdims=True) / (len(parts) * width)
    inverse = lax.rsqrt(mean + EPS)
    tile = units // 2
    for lane in range(0, units, tile):
        gate = up = None
        for block, rows in pieces:
            span = pl.ds(pl.multiple_of(block * width, LANES), width)
            gate_term = jnp.dot(
                rows, gate_ref[span, lane : lane + tile], preferred_element_type=F32
            )
            up_term = jnp.dot(rows, up_ref[span, lane : lane + tile], preferred_element_type=F32)
            gate = gate_term if gate is None else gate + gate_term
            up = up_term if up is None else up + up_term
        gate = gate * inverse
        out_ref[:, lane : lane + tile] = (
            gate / (1.0 + jnp.exp(-gate)) * (up * inverse)
        ).astype(BF16)


def hidden_units(info, pieces, w_gate, w_up, scale):
    parts = [len(piece) for piece in pieces]
    rows = [part for piece in pieces for part in piece]
    tokens = sum(part.shape[0] for part in pieces[0])
    return pl.pallas_call(
        lambda *refs: hidden_kernel(*refs, parts=parts),
        in_specs=[pl.BlockSpec(memory_space=pltpu.SMEM)]
        + [pl.BlockSpec(memory_space=pltpu.VMEM)] * (len(rows) + 3),
        out_shape=jax.ShapeDtypeStruct((tokens, w_gate.shape[1]), BF16),
        compiler_params=pltpu.CompilerParams(vmem_limit_bytes=SMALL_LIMIT),
        cost_estimate=cost(4 * tokens * w_gate.size, [*rows, w_gate, w_up]),
        name="hidden_units",
    )(info, *rows, w_gate, w_up, scale)


def down_kernel(info_ref, a_ref, b_ref, c_ref, d_ref, down_ref, *refs):
    mine = info_ref[0]
    units = a_ref.shape[1]
    tile = 512
    for lane in range(0, down_ref.shape[1], tile):
        total = None
        for index, rows_ref in enumerate((a_ref, b_ref, c_ref, d_ref)):
            start = pl.multiple_of((mine ^ index) * units, units)
            term = jnp.dot(
                rows_ref[...],
                down_ref[pl.ds(start, units), lane : lane + tile],
                preferred_element_type=F32,
            )
            total = term if total is None else total + term
        result = total.astype(BF16)
        if len(refs) == 1:
            refs[0][:, lane : lane + tile] = result
            continue
        before_ref, out_ref = refs
        sources, _, count, _ = out_ref.shape
        here, there = pl.ds(info_ref[1], 1), pl.ds(1 - info_ref[1], 1)
        out_ref[:, here, :, lane : lane + tile] = result.reshape(sources, 1, count, tile)
        out_ref[:, there, :, lane : lane + tile] = before_ref[:, lane : lane + tile].reshape(
            sources, 1, count, tile
        )


def block_outputs(info, hiddens, w_down, before=None):
    tokens = hiddens[0].shape[0]
    columns = w_down.shape[1]
    args = [*hiddens, w_down]
    out_shape = (tokens, columns)
    if before is not None:
        args.append(before)
        out_shape = (tokens // CAP, 2, CAP, columns)
    return pl.pallas_call(
        down_kernel,
        in_specs=[pl.BlockSpec(memory_space=pltpu.SMEM)]
        + [pl.BlockSpec(memory_space=pltpu.VMEM)] * len(args),
        out_shape=jax.ShapeDtypeStruct(out_shape, BF16),
        compiler_params=pltpu.CompilerParams(vmem_limit_bytes=SMALL_LIMIT),
        cost_estimate=cost(2 * tokens * w_down.size, [w_down, w_down]),
        name="block_outputs",
    )(info, *args)


def cost(flops, arrays, transcendentals=0):
    size = sum(array.size * array.dtype.itemsize for array in arrays)
    return pl.CostEstimate(
        flops=flops, bytes_accessed=size, transcendentals=transcendentals
    )


def swap(array, axis):
    return lax.ppermute(array, axis, [(0, 1), (1, 0)])


def shift(array, axis, size, by):
    return lax.ppermute(array, axis, [(i, (i + by) % size) for i in range(size)])


def shift_x(array, by):
    index = [(x % 2) * 2 + x // 2 for x in range(4)]
    return lax.ppermute(
        array, ("xl", "xh"), [(index[x], index[(x + by) % 4]) for x in range(4)]
    )


def on_device(
    queries,
    new_keys,
    new_values,
    cached_key_rows,
    cache_values,
    cache_lengths,
    norm_gain,
    routes,
    gates,
    gate_proj,
    up_proj,
    down_proj,
):
    new_dev, sequences, q_width = queries.shape
    z, y, x_lo, x_hi, core = (lax.axis_index(name) for name in ("z", "y", "xl", "xh", "c"))
    z_size, y_size = lax.axis_size("z"), lax.axis_size("y")
    columns = z_size * y_size
    token_rows = new_dev * sequences
    group = columns // EXPERTS

    def rows_of(cached, new):
        return jnp.concatenate([cached, new], axis=0).reshape(cached.shape[0] + new_dev, -1)

    own_keys = rows_of(cached_key_rows, new_keys)
    own_values = rows_of(cache_values, new_values)
    keys_up, values_up = shift(own_keys, "z", 4, 1), shift(own_values, "z", 4, 1)
    keys_down, values_down = shift(own_keys, "z", 4, -1), shift(own_values, "z", 4, -1)
    keys_far = shift(keys_up, "z", 4, 1)
    values_far = shift(values_down, "z", 4, -1)

    sent = jnp.broadcast_to(
        jnp.transpose(queries, (1, 0, 2))[None], (2 * y_size, sequences, new_dev, q_width)
    )
    everyone = lax.all_to_all(sent, ("y", "xl"), split_axis=0, concat_axis=0, tiled=True)

    basis = [cache_lengths[0], cache_lengths[1], z, y * 2 + x_lo, jnp.int32(4)]
    near_info = jnp.stack(basis + [z, (z + 3) % 4, (z + 1) % 4]).astype(jnp.int32)
    far_info = jnp.stack(basis + [(z + 2) % 4]).astype(jnp.int32)
    state = attend(
        near_info,
        everyone,
        (own_keys, keys_up, keys_down),
        (own_values, values_up, values_down),
    )
    partial = attend(far_info, everyone, (keys_far,), (values_far,), state)
    got = lax.all_to_all(partial, ("y", "xl"), split_axis=0, concat_axis=0, tiled=True)

    gain = norm_gain.astype(F32)
    gain_core = swap(norm_gain, "c")
    gain_pair = jnp.where(
        core == 0, jnp.stack([norm_gain, gain_core]), jnp.stack([gain_core, norm_gain])
    )
    gain_far = swap(gain_pair, "xh")
    gain_all = jnp.where(
        x_hi == 0, jnp.stack([gain_pair, gain_far]), jnp.stack([gain_far, gain_pair])
    ).astype(F32)
    scales = (1.0 / (gain_all * gain_all)).reshape(4, 1, q_width)

    flat_routes = routes.reshape(token_rows * TOPK)
    order = jnp.arange(token_rows * TOPK)
    earlier = (order[None, :] < order[:, None]) & (flat_routes[:, None] == flat_routes[None, :])
    target = flat_routes * CAP + jnp.sum(earlier.astype(jnp.int32), axis=1)
    by_row = target.reshape(new_dev, sequences, TOPK)
    slot_ids = jnp.arange(EXPERTS * CAP).reshape(EXPERTS * CAP, 1, 1, 1)
    hits = slot_ids == by_row[None]
    placing = jnp.transpose(jnp.any(hits, axis=-1), (0, 2, 1)).reshape(EXPERTS * CAP, token_rows)
    weighting = jnp.sum(jnp.where(hits, gates[None], 0.0), axis=-1).reshape(
        EXPERTS, 1, CAP, token_rows
    )

    attended, square, outgoing = merge(
        got, placing.astype(BF16), gain.reshape(1, q_width), columns
    )
    below = ((x_hi * 2 + x_lo + 3) % 4) // 2
    above = ((x_hi * 2 + x_lo + 1) % 4) // 2
    first_info = jnp.stack(
        [below * 2 + core, below * 2 + 1 - core, above * 2 + core, above * 2 + 1 - core]
    ).astype(jnp.int32)
    second_info = jnp.stack(
        [
            x_hi * 2 + core,
            x_hi * 2 + 1 - core,
            (1 - x_hi) * 2 + core,
            (1 - x_hi) * 2 + 1 - core,
        ]
    ).astype(jnp.int32)
    place = jnp.stack([x_hi * 2 + core, x_lo]).astype(jnp.int32)
    rows_back = 2 * columns * CAP
    weighting = jnp.broadcast_to(weighting, (EXPERTS, 2 * group, CAP, token_rows)).reshape(
        rows_back, token_rows
    )
    high_part = weighting.astype(BF16)
    rest = weighting - high_part.astype(F32)
    middle_part = rest.astype(BF16)
    low_part = (rest - middle_part.astype(F32)).astype(BF16)
    table = jnp.concatenate([high_part, middle_part, low_part], axis=1)
    outgoing, scales, first_info, second_info, place, table = lax.optimization_barrier(
        (outgoing, scales, first_info, second_info, place, table)
    )
    own_block = lax.all_to_all(
        outgoing, ("z", "y"), split_axis=0, concat_axis=0, tiled=True
    ).reshape(columns * CAP, q_width)
    w_gate, w_up, w_down = gate_proj[0], up_proj[0], down_proj[0]

    from_below = shift_x(own_block, 1)
    from_above = shift_x(own_block, -1)
    low_half, high_half = halves(from_below, from_above)
    far_low, far_high = shift_x(low_half, 1), shift_x(high_half, -1)
    own_other = swap(own_block, "c")
    below_other = swap(from_below, "c")
    above_other = swap(from_above, "c")

    hidden_first = hidden_units(
        first_info,
        ((from_below,), (below_other,), (from_above,), (above_other,)),
        w_gate,
        w_up,
        scales,
    )
    first_far, first_other = swap(hidden_first, "xh"), swap(hidden_first, "c")
    far_low, far_high, hidden_first = lax.optimization_barrier((far_low, far_high, hidden_first))
    hidden_second = hidden_units(
        second_info,
        (
            (own_block,),
            (own_other,),
            (far_low, far_high),
            (swap(far_low, "c"), swap(far_high, "c")),
        ),
        w_gate,
        w_up,
        scales,
    )
    second_far, second_other = swap(hidden_second, "xh"), swap(hidden_second, "c")
    first_far, second_other = lax.optimization_barrier((first_far, second_other))
    produced_first = block_outputs(
        place, (hidden_first, first_other, first_far, swap(first_far, "c")), w_down
    )
    second_far, produced_first = lax.optimization_barrier((second_far, produced_first))
    produced = block_outputs(
        place,
        (hidden_second, second_other, second_far, swap(second_far, "c")),
        w_down,
        produced_first,
    )

    square, produced = lax.optimization_barrier((square, produced))
    square = square + swap(square, "c")
    square = square + swap(square, "xh")
    inverse = lax.rsqrt(square[:, :1] / (4 * q_width) + EPS).reshape(sequences, new_dev, 1)
    normed = jnp.transpose(attended * inverse * gain, (1, 0, 2))

    returned = lax.all_to_all(
        produced.reshape(2 * columns, CAP, q_width),
        ("z", "y", "xl"),
        split_axis=0,
        concat_axis=0,
        tiled=True,
    )
    mixed = lax.dot_general(
        table,
        returned.reshape(rows_back, q_width),
        (((0,), (0,)), ((), ())),
        preferred_element_type=F32,
    ).reshape(3, token_rows, q_width)
    moe_out = (mixed[0] + mixed[1] + mixed[2]).reshape(new_dev, sequences, q_width)
    return (normed, moe_out)


def solution(mesh):
    fine = Mesh(mesh.devices.reshape(4, 4, 2, 2, 2), ("z", "y", "xl", "xh", "c"))
    ctx = ("z", "y", "xl")
    tp = ("xh", "c")
    split = P(ctx, None, tp)
    placed = (
        split,
        split,
        split,
        split,
        split,
        P(),
        P(tp),
        P(ctx, None, None),
        P(ctx, None, None),
        split,
        split,
        split,
    )
    return jax.shard_map(
        on_device,
        mesh=fine,
        in_specs=placed,
        out_specs=(split, split),
        check_vma=False,
    )
```

```python
import math

import jax
import jax.numpy as jnp
from jax import lax
from jax.experimental import pallas as pl
from jax.experimental.pallas import tpu as pltpu
from jax.sharding import Mesh
from jax.sharding import PartitionSpec as P

HEAD_SIZE = 128
EXPERTS = 8
TOPK = 2
CAP = 16
EPS = 1e-05
DEAD = -1e30
LANES = 128
VMEM_LIMIT = 20 * 1024 * 1024
SMALL_LIMIT = 6 * 1024 * 1024

BF16 = jnp.bfloat16
F32 = jnp.float32


def attention_kernel(info_ref, q_ref, *refs, parts, last):
    key_parts, value_parts = refs[:parts], refs[parts : 2 * parts]
    if last:
        before_ref, before_lse_ref, out_ref, keys_ref, values_ref, lse_ref = refs[2 * parts :]
    else:
        out_ref, out_lse_ref, keys_ref, values_ref = refs[2 * parts :]
    sequence = pl.program_id(0)
    group = pl.program_id(1)
    sources, _, own_rows, width = q_ref.shape
    heads = width // HEAD_SIZE
    tokens = sources * own_rows
    count = key_parts[0].shape[0]
    padded = keys_ref.shape[0]
    cache = count - own_rows
    length = info_ref[sequence]
    z_index = info_ref[2]
    lane_index = info_ref[3]
    planes = info_ref[4]
    multiplier = 1.0 / math.sqrt(HEAD_SIZE)
    flag = 4 * own_rows

    for part in range(parts):
        plane = info_ref[5 + part]
        span = slice(part * count, (part + 1) * count)
        keys_ref[span, :LANES] = key_parts[part][...]
        values_ref[span, :LANES] = value_parts[part][...]
        row = lax.broadcasted_iota(jnp.int32, (count, LANES), 0)
        lane = lax.broadcasted_iota(jnp.int32, (count, LANES), 1)
        first = (plane * sources + lane_index) * cache
        dead = (lane == flag) & (row < cache) & (first + row >= length)
        late = (lane - plane * own_rows == row - cache) & (row >= cache)
        keys_ref[span, LANES:] = jnp.where(dead | late, DEAD, 0.0).astype(BF16)
    rest = padded - parts * count
    if rest:
        lane = lax.broadcasted_iota(jnp.int32, (rest, LANES), 1)
        keys_ref[parts * count :, :LANES] = jnp.zeros((rest, LANES), BF16)
        values_ref[parts * count :, :LANES] = jnp.zeros((rest, LANES), BF16)
        keys_ref[parts * count :, LANES:] = jnp.where(lane == flag, DEAD, 0.0).astype(BF16)
    values_ref[:, LANES:] = jnp.ones((padded, LANES), BF16)

    row = lax.broadcasted_iota(jnp.int32, (tokens, LANES), 0)
    lane = lax.broadcasted_iota(jnp.int32, (tokens, LANES), 1)
    position = z_index * tokens + row
    key_position = ((lane // own_rows) * sources + lane_index) * own_rows + lane % own_rows
    blocked = ((lane < planes * own_rows) & (position < key_position)) | (lane == flag)
    causal = jnp.where(blocked, 1.0, 0.0).astype(BF16)

    together = 2
    packed = None
    for start in range(0, heads, together):
        members = range(start, start + together)
        query = jnp.concatenate(
            [
                q_ref[:, 0, :, h * HEAD_SIZE : (h + 1) * HEAD_SIZE].reshape(tokens, HEAD_SIZE)
                for h in members
            ],
            axis=0,
        )
        wide = jnp.concatenate([query, jnp.concatenate([causal] * together, axis=0)], axis=1)
        scores = lax.dot_general(
            wide, keys_ref[...], (((1,), (1,)), ((), ())), preferred_element_type=F32
        )
        top = jnp.max(scores, axis=1, keepdims=True)
        expo = jnp.exp2((scores - top) * (multiplier * math.log2(math.e)))
        mixed = jnp.dot(expo.astype(BF16), values_ref[...], preferred_element_type=F32)
        total = mixed[:, LANES:]
        result = mixed[:, :LANES] / total
        lse = top * multiplier + jnp.log(total)
        rows = slice(start * tokens, (start + together) * tokens)
        if not last:
            out_ref[0, 0, rows] = result
            out_lse_ref[0, 0, rows] = lse
            continue
        other = before_lse_ref[0, 0, rows]
        peak = jnp.maximum(lse, other)
        here, there = jnp.exp(lse - peak), jnp.exp(other - peak)
        both = here + there
        result = (here * result + there * before_ref[0, 0, rows]) / both
        lse = peak + jnp.log(both)
        for place, h in enumerate(members):
            chosen = slice(place * tokens, (place + 1) * tokens)
            out_ref[:, 0, :, pl.ds(group * width + h * HEAD_SIZE, HEAD_SIZE)] = (
                result[chosen].astype(BF16).reshape(sources, own_rows, HEAD_SIZE)
            )
            mark = (lane % 16 == group * heads + h) & (lane < 48)
            packed = jnp.where(mark, lse[chosen], jnp.zeros((tokens, LANES), F32) if packed is None else packed)

    if last:
        @pl.when(group == 0)
        def _():
            lse_ref[...] = packed

        @pl.when(group == pl.num_programs(1) - 1)
        def _():
            value = lse_ref[...] + packed
            high = value.astype(BF16).astype(F32)
            middle = (value - high).astype(BF16).astype(F32)
            low = value - high - middle
            terms = jnp.where(lane < 16, high, jnp.where(lane < 32, middle, low)).astype(BF16)
            edge = out_ref.shape[3] - LANES
            out_ref[:, 0, :, edge:] = terms.reshape(sources, own_rows, LANES)


def attend(info, queries, keys, values, before=None):
    sources, sequences, own_rows, q_width = queries.shape
    parts = len(keys)
    count = keys[0].shape[0]
    groups = keys[0].shape[1] // HEAD_SIZE // sequences
    width = q_width // groups
    padded = -(-parts * count // LANES) * LANES
    rows = sources * own_rows * width // HEAD_SIZE
    key_spec = pl.BlockSpec((count, HEAD_SIZE), lambda s, g, i: (0, s * groups + g))
    state_spec = pl.BlockSpec((1, 1, rows, HEAD_SIZE), lambda s, g, i: (s, g, 0, 0))
    in_specs = [
        pl.BlockSpec((sources, 1, own_rows, width), lambda s, g, i: (0, s, 0, g))
    ] + [key_spec] * (2 * parts)
    scratch = [pltpu.VMEM((padded, 2 * LANES), BF16), pltpu.VMEM((padded, 2 * LANES), BF16)]
    args = [queries, *keys, *values]
    if before is None:
        state = jax.ShapeDtypeStruct((sequences, groups, rows, HEAD_SIZE), F32)
        out_specs, out_shape = [state_spec] * 2, [state] * 2
    else:
        in_specs += [state_spec] * 2
        args += list(before)
        out_specs = pl.BlockSpec(
            (sources, 1, own_rows, q_width + LANES), lambda s, g, i: (0, s, 0, 0)
        )
        out_shape = jax.ShapeDtypeStruct((sources, sequences, own_rows, q_width + LANES), BF16)
        scratch.append(pltpu.VMEM((sources * own_rows, LANES), F32))
    return pl.pallas_call(
        lambda *refs: attention_kernel(*refs, parts=parts, last=before is not None),
        grid_spec=pltpu.PrefetchScalarGridSpec(
            num_scalar_prefetch=1,
            grid=(sequences, groups),
            in_specs=in_specs,
            out_specs=out_specs,
            scratch_shapes=scratch,
        ),
        out_shape=out_shape,
        compiler_params=pltpu.CompilerParams(vmem_limit_bytes=VMEM_LIMIT),
        cost_estimate=cost(
            8 * sequences * groups * rows * padded * HEAD_SIZE,
            args,
            sequences * groups * rows * padded,
        ),
        name="attend",
    )(info, *args)


def merge_kernel(got_ref, placing_ref, gain_ref, out_ref, square_ref, sent_ref):
    sources, sequences, own_rows, wide = got_ref.shape
    rows = sequences * own_rows
    width = wide - LANES
    parts = got_ref[:, :, :, width:].astype(F32).reshape(sources * rows, LANES)
    lse = parts + pltpu.roll(parts, LANES - 16, 1) + pltpu.roll(parts, LANES - 32, 1)
    lse = lse.reshape(sources, rows, LANES)
    weight = jnp.exp(lse - jnp.max(lse, axis=0, keepdims=True))
    weight = weight / jnp.sum(weight, axis=0, keepdims=True)
    pieces = []
    square = jnp.zeros((rows, LANES), F32)
    for head in range(width // HEAD_SIZE):
        lanes = slice(head * HEAD_SIZE, (head + 1) * HEAD_SIZE)
        merged = jnp.zeros((rows, HEAD_SIZE), F32)
        for source in range(sources):
            part = got_ref[source, :, :, lanes].astype(F32).reshape(rows, HEAD_SIZE)
            merged = merged + weight[source, :, head : head + 1] * part
        out_ref[:, :, lanes] = merged.reshape(sequences, own_rows, HEAD_SIZE)
        square = square + merged * merged
        pieces.append((merged * gain_ref[:, lanes]).astype(BF16))
    square = jnp.sum(square, axis=1, keepdims=True)
    square_ref[...] = jnp.broadcast_to(square, (rows, LANES))
    payload = jnp.concatenate(pieces, axis=1)
    placed = jnp.dot(placing_ref[...], payload, preferred_element_type=F32).astype(BF16)
    placed = placed.reshape(EXPERTS, CAP, width)
    copies = sent_ref.shape[0] // EXPERTS
    for expert in range(EXPERTS):
        for copy in range(copies):
            sent_ref[expert * copies + copy] = placed[expert]


def merge(got, placing, gain, targets):
    sources, sequences, own_rows, wide = got.shape
    width = wide - LANES
    return pl.pallas_call(
        merge_kernel,
        out_shape=[
            jax.ShapeDtypeStruct((sequences, own_rows, width), F32),
            jax.ShapeDtypeStruct((sequences * own_rows, LANES), F32),
            jax.ShapeDtypeStruct((targets, CAP, width), BF16),
        ],
        compiler_params=pltpu.CompilerParams(vmem_limit_bytes=VMEM_LIMIT),
        cost_estimate=cost(8 * got.size, [got, got]),
        name="merge",
    )(got, placing, gain)


def halves_kernel(below_ref, above_ref, low_ref, high_ref):
    middle = low_ref.shape[0]
    low_ref[...] = below_ref[:middle]
    high_ref[...] = above_ref[middle:]


def halves(below, above):
    rows, width = below.shape
    half = jax.ShapeDtypeStruct((rows // 2, width), BF16)
    return pl.pallas_call(
        halves_kernel,
        in_specs=[pl.BlockSpec(memory_space=pltpu.VMEM)] * 2,
        out_specs=[pl.BlockSpec(memory_space=pltpu.VMEM)] * 2,
        out_shape=[half, half],
        compiler_params=pltpu.CompilerParams(vmem_limit_bytes=SMALL_LIMIT),
        cost_estimate=cost(0, [below, above]),
        name="halves",
    )(below, above)


def hidden_kernel(info_ref, *refs, parts):
    rows_refs = refs[: sum(parts)]
    gate_ref, up_ref, scale_ref, out_ref = refs[sum(parts) :]
    units = out_ref.shape[1]
    width = rows_refs[0].shape[1]
    pieces = []
    place = 0
    for index, count in enumerate(parts):
        members = [rows_refs[place + i][...] for i in range(count)]
        place += count
        rows = jnp.concatenate(members, axis=0) if count > 1 else members[0]
        pieces.append((info_ref[index], rows))
    total = None
    for block, rows in pieces:
        for start in range(0, width, LANES):
            part = rows[:, start : start + LANES].astype(F32)
            term = part * part * scale_ref[block, :, start : start + LANES]
            total = term if total is None else total + term
    mean = jnp.sum(total, axis=1, keepdims=True) / (len(parts) * width)
    inverse = lax.rsqrt(mean + EPS)
    tile = units // 2
    for lane in range(0, units, tile):
        gate = up = None
        for block, rows in pieces:
            span = pl.ds(pl.multiple_of(block * width, LANES), width)
            gate_term = jnp.dot(
                rows, gate_ref[span, lane : lane + tile], preferred_element_type=F32
            )
            up_term = jnp.dot(rows, up_ref[span, lane : lane + tile], preferred_element_type=F32)
            gate = gate_term if gate is None else gate + gate_term
            up = up_term if up is None else up + up_term
        gate = gate * inverse
        out_ref[:, lane : lane + tile] = (
            gate / (1.0 + jnp.exp(-gate)) * (up * inverse)
        ).astype(BF16)


def hidden_units(info, pieces, w_gate, w_up, scale):
    parts = [len(piece) for piece in pieces]
    rows = [part for piece in pieces for part in piece]
    tokens = sum(part.shape[0] for part in pieces[0])
    return pl.pallas_call(
        lambda *refs: hidden_kernel(*refs, parts=parts),
        in_specs=[pl.BlockSpec(memory_space=pltpu.SMEM)]
        + [pl.BlockSpec(memory_space=pltpu.VMEM)] * (len(rows) + 3),
        out_shape=jax.ShapeDtypeStruct((tokens, w_gate.shape[1]), BF16),
        compiler_params=pltpu.CompilerParams(vmem_limit_bytes=SMALL_LIMIT),
        cost_estimate=cost(4 * tokens * w_gate.size, [*rows, w_gate, w_up]),
        name="hidden_units",
    )(info, *rows, w_gate, w_up, scale)


def down_kernel(info_ref, *refs):
    first_refs, second_refs, down_ref, out_ref = refs[:4], refs[4:8], refs[8], refs[9]
    units = first_refs[0].shape[1]
    sources, _, count, columns = out_ref.shape
    middle = sources * count
    tile = 512
    pieces = []
    for index, (first_ref, second_ref) in enumerate(zip(first_refs, second_refs)):
        start = pl.multiple_of((info_ref[0] ^ index) * units, units)
        pieces.append((start, jnp.concatenate([first_ref[...], second_ref[...]], axis=0)))
    here, there = pl.ds(info_ref[1], 1), pl.ds(1 - info_ref[1], 1)
    for lane in range(0, columns, tile):
        total = None
        for start, rows in pieces:
            term = jnp.dot(
                rows,
                down_ref[pl.ds(start, units), lane : lane + tile],
                preferred_element_type=F32,
            )
            total = term if total is None else total + term
        result = total.astype(BF16)
        shape = (sources, 1, count, tile)
        out_ref[:, there, :, lane : lane + tile] = result[:middle].reshape(shape)
        out_ref[:, here, :, lane : lane + tile] = result[middle:].reshape(shape)


def block_outputs(info, first, second, w_down):
    tokens = first[0].shape[0]
    columns = w_down.shape[1]
    args = [*first, *second, w_down]
    return pl.pallas_call(
        down_kernel,
        in_specs=[pl.BlockSpec(memory_space=pltpu.SMEM)]
        + [pl.BlockSpec(memory_space=pltpu.VMEM)] * len(args),
        out_shape=jax.ShapeDtypeStruct((tokens // CAP, 2, CAP, columns), BF16),
        compiler_params=pltpu.CompilerParams(vmem_limit_bytes=SMALL_LIMIT),
        cost_estimate=cost(4 * tokens * w_down.size, [w_down, w_down]),
        name="block_outputs",
    )(info, *args)


def cost(flops, arrays, transcendentals=0):
    size = sum(array.size * array.dtype.itemsize for array in arrays)
    return pl.CostEstimate(
        flops=flops, bytes_accessed=size, transcendentals=transcendentals
    )


def swap(array, axis):
    return lax.ppermute(array, axis, [(0, 1), (1, 0)])


def shift(array, axis, size, by):
    return lax.ppermute(array, axis, [(i, (i + by) % size) for i in range(size)])


def shift_x(array, by):
    index = [(x % 2) * 2 + x // 2 for x in range(4)]
    return lax.ppermute(
        array, ("xl", "xh"), [(index[x], index[(x + by) % 4]) for x in range(4)]
    )


def on_device(
    queries,
    new_keys,
    new_values,
    cached_key_rows,
    cache_values,
    cache_lengths,
    norm_gain,
    routes,
    gates,
    gate_proj,
    up_proj,
    down_proj,
):
    new_dev, sequences, q_width = queries.shape
    z, y, x_lo, x_hi, core = (lax.axis_index(name) for name in ("z", "y", "xl", "xh", "c"))
    z_size, y_size = lax.axis_size("z"), lax.axis_size("y")
    columns = z_size * y_size
    token_rows = new_dev * sequences
    group = columns // EXPERTS

    def rows_of(cached, new):
        return jnp.concatenate([cached, new], axis=0).reshape(cached.shape[0] + new_dev, -1)

    own_keys = rows_of(cached_key_rows, new_keys)
    own_values = rows_of(cache_values, new_values)
    keys_up, values_up = shift(own_keys, "z", 4, 1), shift(own_values, "z", 4, 1)
    keys_down, values_down = shift(own_keys, "z", 4, -1), shift(own_values, "z", 4, -1)
    keys_far = shift(keys_up, "z", 4, 1)
    values_far = shift(values_down, "z", 4, -1)

    sent = jnp.broadcast_to(
        jnp.transpose(queries, (1, 0, 2))[None], (2 * y_size, sequences, new_dev, q_width)
    )
    everyone = lax.all_to_all(sent, ("y", "xl"), split_axis=0, concat_axis=0, tiled=True)

    basis = [cache_lengths[0], cache_lengths[1], z, y * 2 + x_lo, jnp.int32(4)]
    near_info = jnp.stack(basis + [z, (z + 3) % 4, (z + 1) % 4]).astype(jnp.int32)
    far_info = jnp.stack(basis + [(z + 2) % 4]).astype(jnp.int32)
    state = attend(
        near_info,
        everyone,
        (own_keys, keys_up, keys_down),
        (own_values, values_up, values_down),
    )
    partial = attend(far_info, everyone, (keys_far,), (values_far,), state)
    got = lax.all_to_all(partial, ("y", "xl"), split_axis=0, concat_axis=0, tiled=True)

    gain = norm_gain.astype(F32)
    gain_core = swap(norm_gain, "c")
    gain_pair = jnp.where(
        core == 0, jnp.stack([norm_gain, gain_core]), jnp.stack([gain_core, norm_gain])
    )
    gain_far = swap(gain_pair, "xh")
    gain_all = jnp.where(
        x_hi == 0, jnp.stack([gain_pair, gain_far]), jnp.stack([gain_far, gain_pair])
    ).astype(F32)
    scales = (1.0 / (gain_all * gain_all)).reshape(4, 1, q_width)

    flat_routes = routes.reshape(token_rows * TOPK)
    order = jnp.arange(token_rows * TOPK)
    earlier = (order[None, :] < order[:, None]) & (flat_routes[:, None] == flat_routes[None, :])
    target = flat_routes * CAP + jnp.sum(earlier.astype(jnp.int32), axis=1)
    by_row = target.reshape(new_dev, sequences, TOPK)
    slot_ids = jnp.arange(EXPERTS * CAP).reshape(EXPERTS * CAP, 1, 1, 1)
    hits = slot_ids == by_row[None]
    placing = jnp.transpose(jnp.any(hits, axis=-1), (0, 2, 1)).reshape(EXPERTS * CAP, token_rows)
    weighting = jnp.sum(jnp.where(hits, gates[None], 0.0), axis=-1).reshape(
        EXPERTS, 1, CAP, token_rows
    )

    attended, square, outgoing = merge(
        got, placing.astype(BF16), gain.reshape(1, q_width), columns
    )
    below = ((x_hi * 2 + x_lo + 3) % 4) // 2
    above = ((x_hi * 2 + x_lo + 1) % 4) // 2
    first_info = jnp.stack(
        [below * 2 + core, below * 2 + 1 - core, above * 2 + core, above * 2 + 1 - core]
    ).astype(jnp.int32)
    second_info = jnp.stack(
        [
            x_hi * 2 + core,
            x_hi * 2 + 1 - core,
            (1 - x_hi) * 2 + core,
            (1 - x_hi) * 2 + 1 - core,
        ]
    ).astype(jnp.int32)
    place = jnp.stack([x_hi * 2 + core, x_lo]).astype(jnp.int32)
    rows_back = 2 * columns * CAP
    weighting = jnp.broadcast_to(weighting, (EXPERTS, 2 * group, CAP, token_rows)).reshape(
        rows_back, token_rows
    )
    high_part = weighting.astype(BF16)
    rest = weighting - high_part.astype(F32)
    middle_part = rest.astype(BF16)
    low_part = (rest - middle_part.astype(F32)).astype(BF16)
    table = jnp.concatenate([high_part, middle_part, low_part], axis=1)
    outgoing, scales, first_info, second_info, place, table = lax.optimization_barrier(
        (outgoing, scales, first_info, second_info, place, table)
    )
    own_block = lax.all_to_all(
        outgoing, ("z", "y"), split_axis=0, concat_axis=0, tiled=True
    ).reshape(columns * CAP, q_width)
    w_gate, w_up, w_down = gate_proj[0], up_proj[0], down_proj[0]

    from_below = shift_x(own_block, 1)
    from_above = shift_x(own_block, -1)
    low_half, high_half = halves(from_below, from_above)
    far_low, far_high = shift_x(low_half, 1), shift_x(high_half, -1)
    own_other = swap(own_block, "c")
    below_other = swap(from_below, "c")
    above_other = swap(from_above, "c")

    hidden_first = hidden_units(
        first_info,
        ((from_below,), (below_other,), (from_above,), (above_other,)),
        w_gate,
        w_up,
        scales,
    )
    first_far, first_other = swap(hidden_first, "xh"), swap(hidden_first, "c")
    far_low, far_high, hidden_first = lax.optimization_barrier((far_low, far_high, hidden_first))
    hidden_second = hidden_units(
        second_info,
        (
            (own_block,),
            (own_other,),
            (far_low, far_high),
            (swap(far_low, "c"), swap(far_high, "c")),
        ),
        w_gate,
        w_up,
        scales,
    )
    second_far, second_other = swap(hidden_second, "xh"), swap(hidden_second, "c")
    produced = block_outputs(
        place,
        (hidden_first, first_other, first_far, swap(first_far, "c")),
        (hidden_second, second_other, second_far, swap(second_far, "c")),
        w_down,
    )

    square, produced = lax.optimization_barrier((square, produced))
    square = square + swap(square, "c")
    square = square + swap(square, "xh")
    inverse = lax.rsqrt(square[:, :1] / (4 * q_width) + EPS).reshape(sequences, new_dev, 1)
    normed = jnp.transpose(attended * inverse * gain, (1, 0, 2))

    returned = lax.all_to_all(
        produced.reshape(2 * columns, CAP, q_width),
        ("z", "y", "xl"),
        split_axis=0,
        concat_axis=0,
        tiled=True,
    )
    mixed = lax.dot_general(
        table,
        returned.reshape(rows_back, q_width),
        (((0,), (0,)), ((), ())),
        preferred_element_type=F32,
    ).reshape(3, token_rows, q_width)
    moe_out = (mixed[0] + mixed[1] + mixed[2]).reshape(new_dev, sequences, q_width)
    return (normed, moe_out)


def solution(mesh):
    fine = Mesh(mesh.devices.reshape(4, 4, 2, 2, 2), ("z", "y", "xl", "xh", "c"))
    ctx = ("z", "y", "xl")
    tp = ("xh", "c")
    split = P(ctx, None, tp)
    placed = (
        split,
        split,
        split,
        split,
        split,
        P(),
        P(tp),
        P(ctx, None, None),
        P(ctx, None, None),
        split,
        split,
        split,
    )
    return jax.shard_map(
        on_device,
        mesh=fine,
        in_specs=placed,
        out_specs=(split, split),
        check_vma=False,
    )
```

```python
import math

import jax
import jax.numpy as jnp
from jax import lax
from jax.experimental import pallas as pl
from jax.experimental.pallas import tpu as pltpu
from jax.sharding import Mesh
from jax.sharding import PartitionSpec as P

HEAD_SIZE = 128
EXPERTS = 8
TOPK = 2
CAP = 16
EPS = 1e-05
DEAD = -1e30
LANES = 128
VMEM_LIMIT = 20 * 1024 * 1024
SMALL_LIMIT = 6 * 1024 * 1024

BF16 = jnp.bfloat16
F32 = jnp.float32


def attention_kernel(info_ref, q_ref, *refs, parts, last):
    key_parts, value_parts = refs[:parts], refs[parts : 2 * parts]
    if last:
        before_ref, before_lse_ref, out_ref, keys_ref, values_ref, lse_ref = refs[2 * parts :]
    else:
        out_ref, out_lse_ref, keys_ref, values_ref = refs[2 * parts :]
    sequence = pl.program_id(0)
    group = pl.program_id(1)
    sources, _, own_rows, width = q_ref.shape
    heads = width // HEAD_SIZE
    tokens = sources * own_rows
    count = key_parts[0].shape[0]
    padded = keys_ref.shape[0]
    cache = count - own_rows
    length = info_ref[sequence]
    z_index = info_ref[2]
    lane_index = info_ref[3]
    planes = info_ref[4]
    multiplier = 1.0 / math.sqrt(HEAD_SIZE)
    flag = 4 * own_rows

    for part in range(parts):
        plane = info_ref[5 + part]
        span = slice(part * count, (part + 1) * count)
        keys_ref[span, :LANES] = key_parts[part][...]
        values_ref[span, :LANES] = value_parts[part][...]
        row = lax.broadcasted_iota(jnp.int32, (count, LANES), 0)
        lane = lax.broadcasted_iota(jnp.int32, (count, LANES), 1)
        first = (plane * sources + lane_index) * cache
        dead = (lane == flag) & (row < cache) & (first + row >= length)
        late = (lane - plane * own_rows == row - cache) & (row >= cache)
        keys_ref[span, LANES:] = jnp.where(dead | late, DEAD, 0.0).astype(BF16)
    rest = padded - parts * count
    if rest:
        lane = lax.broadcasted_iota(jnp.int32, (rest, LANES), 1)
        keys_ref[parts * count :, :LANES] = jnp.zeros((rest, LANES), BF16)
        values_ref[parts * count :, :LANES] = jnp.zeros((rest, LANES), BF16)
        keys_ref[parts * count :, LANES:] = jnp.where(lane == flag, DEAD, 0.0).astype(BF16)
    values_ref[:, LANES:] = jnp.ones((padded, LANES), BF16)

    row = lax.broadcasted_iota(jnp.int32, (tokens, LANES), 0)
    lane = lax.broadcasted_iota(jnp.int32, (tokens, LANES), 1)
    position = z_index * tokens + row
    key_position = ((lane // own_rows) * sources + lane_index) * own_rows + lane % own_rows
    blocked = ((lane < planes * own_rows) & (position < key_position)) | (lane == flag)
    causal = jnp.where(blocked, 1.0, 0.0).astype(BF16)

    together = 2
    packed = None
    for start in range(0, heads, together):
        members = range(start, start + together)
        query = jnp.concatenate(
            [
                q_ref[:, 0, :, h * HEAD_SIZE : (h + 1) * HEAD_SIZE].reshape(tokens, HEAD_SIZE)
                for h in members
            ],
            axis=0,
        )
        wide = jnp.concatenate([query, jnp.concatenate([causal] * together, axis=0)], axis=1)
        scores = lax.dot_general(
            wide, keys_ref[...], (((1,), (1,)), ((), ())), preferred_element_type=F32
        )
        top = jnp.max(scores, axis=1, keepdims=True)
        expo = jnp.exp2((scores - top) * (multiplier * math.log2(math.e)))
        mixed = jnp.dot(expo.astype(BF16), values_ref[...], preferred_element_type=F32)
        total = mixed[:, LANES:]
        result = mixed[:, :LANES] / total
        lse = top * multiplier + jnp.log(total)
        rows = slice(start * tokens, (start + together) * tokens)
        if not last:
            out_ref[0, 0, rows] = result
            out_lse_ref[0, 0, rows] = lse
            continue
        other = before_lse_ref[0, 0, rows]
        peak = jnp.maximum(lse, other)
        here, there = jnp.exp(lse - peak), jnp.exp(other - peak)
        both = here + there
        result = (here * result + there * before_ref[0, 0, rows]) / both
        lse = peak + jnp.log(both)
        for place, h in enumerate(members):
            chosen = slice(place * tokens, (place + 1) * tokens)
            out_ref[:, 0, :, pl.ds(group * width + h * HEAD_SIZE, HEAD_SIZE)] = (
                result[chosen].astype(BF16).reshape(sources, own_rows, HEAD_SIZE)
            )
            mark = (lane % 16 == group * heads + h) & (lane < 48)
            packed = jnp.where(mark, lse[chosen], jnp.zeros((tokens, LANES), F32) if packed is None else packed)

    if last:
        @pl.when(group == 0)
        def _():
            lse_ref[...] = packed

        @pl.when(group == pl.num_programs(1) - 1)
        def _():
            value = lse_ref[...] + packed
            high = value.astype(BF16).astype(F32)
            middle = (value - high).astype(BF16).astype(F32)
            low = value - high - middle
            terms = jnp.where(lane < 16, high, jnp.where(lane < 32, middle, low)).astype(BF16)
            edge = out_ref.shape[3] - LANES
            out_ref[:, 0, :, edge:] = terms.reshape(sources, own_rows, LANES)


def attend(info, queries, keys, values, before=None):
    sources, sequences, own_rows, q_width = queries.shape
    parts = len(keys)
    count = keys[0].shape[0]
    groups = keys[0].shape[1] // HEAD_SIZE // sequences
    width = q_width // groups
    padded = -(-parts * count // LANES) * LANES
    rows = sources * own_rows * width // HEAD_SIZE
    key_spec = pl.BlockSpec((count, HEAD_SIZE), lambda s, g, i: (0, s * groups + g))
    state_spec = pl.BlockSpec((1, 1, rows, HEAD_SIZE), lambda s, g, i: (s, g, 0, 0))
    in_specs = [
        pl.BlockSpec((sources, 1, own_rows, width), lambda s, g, i: (0, s, 0, g))
    ] + [key_spec] * (2 * parts)
    scratch = [pltpu.VMEM((padded, 2 * LANES), BF16), pltpu.VMEM((padded, 2 * LANES), BF16)]
    args = [queries, *keys, *values]
    if before is None:
        state = jax.ShapeDtypeStruct((sequences, groups, rows, HEAD_SIZE), F32)
        out_specs, out_shape = [state_spec] * 2, [state] * 2
    else:
        in_specs += [state_spec] * 2
        args += list(before)
        out_specs = pl.BlockSpec(
            (sources, 1, own_rows, q_width + LANES), lambda s, g, i: (0, s, 0, 0)
        )
        out_shape = jax.ShapeDtypeStruct((sources, sequences, own_rows, q_width + LANES), BF16)
        scratch.append(pltpu.VMEM((sources * own_rows, LANES), F32))
    return pl.pallas_call(
        lambda *refs: attention_kernel(*refs, parts=parts, last=before is not None),
        grid_spec=pltpu.PrefetchScalarGridSpec(
            num_scalar_prefetch=1,
            grid=(sequences, groups),
            in_specs=in_specs,
            out_specs=out_specs,
            scratch_shapes=scratch,
        ),
        out_shape=out_shape,
        compiler_params=pltpu.CompilerParams(vmem_limit_bytes=VMEM_LIMIT),
        cost_estimate=cost(
            8 * sequences * groups * rows * padded * HEAD_SIZE,
            args,
            sequences * groups * rows * padded,
        ),
        name="attend",
    )(info, *args)


def merge_kernel(got_ref, placing_ref, gain_ref, out_ref, square_ref, sent_ref):
    sources, sequences, own_rows, wide = got_ref.shape
    rows = sequences * own_rows
    width = wide - LANES
    parts = got_ref[:, :, :, width:].astype(F32).reshape(sources * rows, LANES)
    lse = parts + pltpu.roll(parts, LANES - 16, 1) + pltpu.roll(parts, LANES - 32, 1)
    lse = lse.reshape(sources, rows, LANES)
    weight = jnp.exp(lse - jnp.max(lse, axis=0, keepdims=True))
    weight = weight / jnp.sum(weight, axis=0, keepdims=True)
    pieces = []
    square = jnp.zeros((rows, LANES), F32)
    for head in range(width // HEAD_SIZE):
        lanes = slice(head * HEAD_SIZE, (head + 1) * HEAD_SIZE)
        merged = jnp.zeros((rows, HEAD_SIZE), F32)
        for source in range(sources):
            part = got_ref[source, :, :, lanes].astype(F32).reshape(rows, HEAD_SIZE)
            merged = merged + weight[source, :, head : head + 1] * part
        out_ref[:, :, lanes] = merged.reshape(sequences, own_rows, HEAD_SIZE)
        square = square + merged * merged
        pieces.append((merged * gain_ref[:, lanes]).astype(BF16))
    square = jnp.sum(square, axis=1, keepdims=True)
    square_ref[...] = jnp.broadcast_to(square, (rows, LANES))
    payload = jnp.concatenate(pieces, axis=1)
    placed = jnp.dot(placing_ref[...], payload, preferred_element_type=F32).astype(BF16)
    placed = placed.reshape(EXPERTS, CAP, width)
    copies = sent_ref.shape[0] // EXPERTS
    for expert in range(EXPERTS):
        for copy in range(copies):
            sent_ref[expert * copies + copy] = placed[expert]


def merge(got, placing, gain, targets):
    sources, sequences, own_rows, wide = got.shape
    width = wide - LANES
    return pl.pallas_call(
        merge_kernel,
        out_shape=[
            jax.ShapeDtypeStruct((sequences, own_rows, width), F32),
            jax.ShapeDtypeStruct((sequences * own_rows, LANES), F32),
            jax.ShapeDtypeStruct((targets, CAP, width), BF16),
        ],
        compiler_params=pltpu.CompilerParams(vmem_limit_bytes=VMEM_LIMIT),
        cost_estimate=cost(8 * got.size, [got, got]),
        name="merge",
    )(got, placing, gain)


def bring_kernel(*refs):
    refs[-1][...] = jnp.zeros_like(refs[-1])


def bring(token, *arrays):
    return pl.pallas_call(
        bring_kernel,
        in_specs=[pl.BlockSpec(memory_space=pl.ANY)]
        + [pl.BlockSpec(memory_space=pltpu.VMEM)] * len(arrays),
        out_specs=pl.BlockSpec(memory_space=pltpu.VMEM),
        out_shape=jax.ShapeDtypeStruct((8, LANES), F32),
        compiler_params=pltpu.CompilerParams(vmem_limit_bytes=1024 * 1024),
        cost_estimate=cost(0, arrays),
        name="bring",
    )(token, *arrays)


def halves_kernel(below_ref, above_ref, token_ref, low_ref, high_ref):
    middle = low_ref.shape[0]
    low_ref[...] = below_ref[:middle]
    high_ref[...] = above_ref[middle:]


def halves(below, above, token):
    rows, width = below.shape
    half = jax.ShapeDtypeStruct((rows // 2, width), BF16)
    return pl.pallas_call(
        halves_kernel,
        in_specs=[pl.BlockSpec(memory_space=pltpu.VMEM)] * 3,
        out_specs=[pl.BlockSpec(memory_space=pltpu.VMEM)] * 2,
        out_shape=[half, half],
        compiler_params=pltpu.CompilerParams(vmem_limit_bytes=SMALL_LIMIT),
        cost_estimate=cost(0, [below, above]),
        name="halves",
    )(below, above, token)


def hidden_kernel(info_ref, *refs, parts):
    rows_refs = refs[: sum(parts)]
    gate_ref, up_ref, scale_ref, out_ref = refs[sum(parts) :]
    units = out_ref.shape[1]
    width = rows_refs[0].shape[1]
    pieces = []
    place = 0
    for index, count in enumerate(parts):
        members = [rows_refs[place + i][...] for i in range(count)]
        place += count
        rows = jnp.concatenate(members, axis=0) if count > 1 else members[0]
        pieces.append((info_ref[index], rows))
    total = None
    for block, rows in pieces:
        for start in range(0, width, LANES):
            part = rows[:, start : start + LANES].astype(F32)
            term = part * part * scale_ref[block, :, start : start + LANES]
            total = term if total is None else total + term
    mean = jnp.sum(total, axis=1, keepdims=True) / (len(parts) * width)
    inverse = lax.rsqrt(mean + EPS)
    tile = units // 2
    for lane in range(0, units, tile):
        gate = up = None
        for block, rows in pieces:
            span = pl.ds(pl.multiple_of(block * width, LANES), width)
            gate_term = jnp.dot(
                rows, gate_ref[span, lane : lane + tile], preferred_element_type=F32
            )
            up_term = jnp.dot(rows, up_ref[span, lane : lane + tile], preferred_element_type=F32)
            gate = gate_term if gate is None else gate + gate_term
            up = up_term if up is None else up + up_term
        gate = gate * inverse
        out_ref[:, lane : lane + tile] = (
            gate / (1.0 + jnp.exp(-gate)) * (up * inverse)
        ).astype(BF16)


def hidden_units(info, pieces, w_gate, w_up, scale):
    parts = [len(piece) for piece in pieces]
    rows = [part for piece in pieces for part in piece]
    tokens = sum(part.shape[0] for part in pieces[0])
    return pl.pallas_call(
        lambda *refs: hidden_kernel(*refs, parts=parts),
        in_specs=[pl.BlockSpec(memory_space=pltpu.SMEM)]
        + [pl.BlockSpec(memory_space=pltpu.VMEM)] * (len(rows) + 3),
        out_shape=jax.ShapeDtypeStruct((tokens, w_gate.shape[1]), BF16),
        compiler_params=pltpu.CompilerParams(vmem_limit_bytes=SMALL_LIMIT),
        cost_estimate=cost(4 * tokens * w_gate.size, [*rows, w_gate, w_up]),
        name="hidden_units",
    )(info, *rows, w_gate, w_up, scale)


def down_kernel(info_ref, *refs):
    first_refs, second_refs, down_ref, out_ref = refs[:4], refs[4:8], refs[8], refs[9]
    units = first_refs[0].shape[1]
    sources, _, count, columns = out_ref.shape
    middle = sources * count
    tile = 512
    pieces = []
    for index, (first_ref, second_ref) in enumerate(zip(first_refs, second_refs)):
        start = pl.multiple_of((info_ref[0] ^ index) * units, units)
        pieces.append((start, jnp.concatenate([first_ref[...], second_ref[...]], axis=0)))
    here, there = pl.ds(info_ref[1], 1), pl.ds(1 - info_ref[1], 1)
    for lane in range(0, columns, tile):
        total = None
        for start, rows in pieces:
            term = jnp.dot(
                rows,
                down_ref[pl.ds(start, units), lane : lane + tile],
                preferred_element_type=F32,
            )
            total = term if total is None else total + term
        result = total.astype(BF16)
        shape = (sources, 1, count, tile)
        out_ref[:, there, :, lane : lane + tile] = result[:middle].reshape(shape)
        out_ref[:, here, :, lane : lane + tile] = result[middle:].reshape(shape)


def block_outputs(info, first, second, w_down):
    tokens = first[0].shape[0]
    columns = w_down.shape[1]
    args = [*first, *second, w_down]
    return pl.pallas_call(
        down_kernel,
        in_specs=[pl.BlockSpec(memory_space=pltpu.SMEM)]
        + [pl.BlockSpec(memory_space=pltpu.VMEM)] * len(args),
        out_shape=jax.ShapeDtypeStruct((tokens // CAP, 2, CAP, columns), BF16),
        compiler_params=pltpu.CompilerParams(vmem_limit_bytes=SMALL_LIMIT),
        cost_estimate=cost(4 * tokens * w_down.size, [w_down, w_down]),
        name="block_outputs",
    )(info, *args)


def cost(flops, arrays, transcendentals=0):
    size = sum(array.size * array.dtype.itemsize for array in arrays)
    return pl.CostEstimate(
        flops=flops, bytes_accessed=size, transcendentals=transcendentals
    )


def swap(array, axis):
    return lax.ppermute(array, axis, [(0, 1), (1, 0)])


def shift(array, axis, size, by):
    return lax.ppermute(array, axis, [(i, (i + by) % size) for i in range(size)])


def shift_x(array, by):
    index = [(x % 2) * 2 + x // 2 for x in range(4)]
    return lax.ppermute(
        array, ("xl", "xh"), [(index[x], index[(x + by) % 4]) for x in range(4)]
    )


def on_device(
    queries,
    new_keys,
    new_values,
    cached_key_rows,
    cache_values,
    cache_lengths,
    norm_gain,
    routes,
    gates,
    gate_proj,
    up_proj,
    down_proj,
):
    new_dev, sequences, q_width = queries.shape
    z, y, x_lo, x_hi, core = (lax.axis_index(name) for name in ("z", "y", "xl", "xh", "c"))
    z_size, y_size = lax.axis_size("z"), lax.axis_size("y")
    columns = z_size * y_size
    token_rows = new_dev * sequences
    group = columns // EXPERTS

    def rows_of(cached, new):
        return jnp.concatenate([cached, new], axis=0).reshape(cached.shape[0] + new_dev, -1)

    own_keys = rows_of(cached_key_rows, new_keys)
    own_values = rows_of(cache_values, new_values)
    keys_up, values_up = shift(own_keys, "z", 4, 1), shift(own_values, "z", 4, 1)
    keys_down, values_down = shift(own_keys, "z", 4, -1), shift(own_values, "z", 4, -1)
    keys_far = shift(keys_up, "z", 4, 1)
    values_far = shift(values_down, "z", 4, -1)

    sent = jnp.broadcast_to(
        jnp.transpose(queries, (1, 0, 2))[None], (2 * y_size, sequences, new_dev, q_width)
    )
    everyone = lax.all_to_all(sent, ("y", "xl"), split_axis=0, concat_axis=0, tiled=True)

    basis = [cache_lengths[0], cache_lengths[1], z, y * 2 + x_lo, jnp.int32(4)]
    near_info = jnp.stack(basis + [z, (z + 3) % 4, (z + 1) % 4]).astype(jnp.int32)
    far_info = jnp.stack(basis + [(z + 2) % 4]).astype(jnp.int32)
    state = attend(
        near_info,
        everyone,
        (own_keys, keys_up, keys_down),
        (own_values, values_up, values_down),
    )
    partial = attend(far_info, everyone, (keys_far,), (values_far,), state)
    got = lax.all_to_all(partial, ("y", "xl"), split_axis=0, concat_axis=0, tiled=True)

    gain = norm_gain.astype(F32)
    gain_core = swap(norm_gain, "c")
    gain_pair = jnp.where(
        core == 0, jnp.stack([norm_gain, gain_core]), jnp.stack([gain_core, norm_gain])
    )
    gain_far = swap(gain_pair, "xh")
    gain_all = jnp.where(
        x_hi == 0, jnp.stack([gain_pair, gain_far]), jnp.stack([gain_far, gain_pair])
    ).astype(F32)
    scales = (1.0 / (gain_all * gain_all)).reshape(4, 1, q_width)

    flat_routes = routes.reshape(token_rows * TOPK)
    order = jnp.arange(token_rows * TOPK)
    earlier = (order[None, :] < order[:, None]) & (flat_routes[:, None] == flat_routes[None, :])
    target = flat_routes * CAP + jnp.sum(earlier.astype(jnp.int32), axis=1)
    by_row = target.reshape(new_dev, sequences, TOPK)
    slot_ids = jnp.arange(EXPERTS * CAP).reshape(EXPERTS * CAP, 1, 1, 1)
    hits = slot_ids == by_row[None]
    placing = jnp.transpose(jnp.any(hits, axis=-1), (0, 2, 1)).reshape(EXPERTS * CAP, token_rows)
    weighting = jnp.sum(jnp.where(hits, gates[None], 0.0), axis=-1).reshape(
        EXPERTS, 1, CAP, token_rows
    )

    attended, square, outgoing = merge(
        got, placing.astype(BF16), gain.reshape(1, q_width), columns
    )
    below = ((x_hi * 2 + x_lo + 3) % 4) // 2
    above = ((x_hi * 2 + x_lo + 1) % 4) // 2
    first_info = jnp.stack(
        [below * 2 + core, below * 2 + 1 - core, above * 2 + core, above * 2 + 1 - core]
    ).astype(jnp.int32)
    second_info = jnp.stack(
        [
            x_hi * 2 + core,
            x_hi * 2 + 1 - core,
            (1 - x_hi) * 2 + core,
            (1 - x_hi) * 2 + 1 - core,
        ]
    ).astype(jnp.int32)
    place = jnp.stack([x_hi * 2 + core, x_lo]).astype(jnp.int32)
    rows_back = 2 * columns * CAP
    weighting = jnp.broadcast_to(weighting, (EXPERTS, 2 * group, CAP, token_rows)).reshape(
        rows_back, token_rows
    )
    high_part = weighting.astype(BF16)
    rest = weighting - high_part.astype(F32)
    middle_part = rest.astype(BF16)
    low_part = (rest - middle_part.astype(F32)).astype(BF16)
    table = jnp.concatenate([high_part, middle_part, low_part], axis=1)
    outgoing, scales, first_info, second_info, place, table = lax.optimization_barrier(
        (outgoing, scales, first_info, second_info, place, table)
    )
    own_block = lax.all_to_all(
        outgoing, ("z", "y"), split_axis=0, concat_axis=0, tiled=True
    ).reshape(columns * CAP, q_width)
    w_gate, w_up, w_down = gate_proj[0], up_proj[0], down_proj[0]

    from_below = shift_x(own_block, 1)
    from_above = shift_x(own_block, -1)
    brought = bring(own_block, w_gate, w_up)
    from_below, from_above, brought = lax.optimization_barrier((from_below, from_above, brought))
    low_half, high_half = halves(from_below, from_above, brought)
    far_low, far_high = shift_x(low_half, 1), shift_x(high_half, -1)
    own_other = swap(own_block, "c")
    below_other = swap(from_below, "c")
    above_other = swap(from_above, "c")

    hidden_first = hidden_units(
        first_info,
        ((from_below,), (below_other,), (from_above,), (above_other,)),
        w_gate,
        w_up,
        scales,
    )
    first_far, first_other = swap(hidden_first, "xh"), swap(hidden_first, "c")
    far_low, far_high, hidden_first = lax.optimization_barrier((far_low, far_high, hidden_first))
    hidden_second = hidden_units(
        second_info,
        (
            (own_block,),
            (own_other,),
            (far_low, far_high),
            (swap(far_low, "c"), swap(far_high, "c")),
        ),
        w_gate,
        w_up,
        scales,
    )
    second_far, second_other = swap(hidden_second, "xh"), swap(hidden_second, "c")
    produced = block_outputs(
        place,
        (hidden_first, first_other, first_far, swap(first_far, "c")),
        (hidden_second, second_other, second_far, swap(second_far, "c")),
        w_down,
    )

    square, produced = lax.optimization_barrier((square, produced))
    square = square + swap(square, "c")
    square = square + swap(square, "xh")
    inverse = lax.rsqrt(square[:, :1] / (4 * q_width) + EPS).reshape(sequences, new_dev, 1)
    normed = jnp.transpose(attended * inverse * gain, (1, 0, 2))

    returned = lax.all_to_all(
        produced.reshape(2 * columns, CAP, q_width),
        ("z", "y", "xl"),
        split_axis=0,
        concat_axis=0,
        tiled=True,
    )
    mixed = lax.dot_general(
        table,
        returned.reshape(rows_back, q_width),
        (((0,), (0,)), ((), ())),
        preferred_element_type=F32,
    ).reshape(3, token_rows, q_width)
    moe_out = (mixed[0] + mixed[1] + mixed[2]).reshape(new_dev, sequences, q_width)
    return (normed, moe_out)


def solution(mesh):
    fine = Mesh(mesh.devices.reshape(4, 4, 2, 2, 2), ("z", "y", "xl", "xh", "c"))
    ctx = ("z", "y", "xl")
    tp = ("xh", "c")
    split = P(ctx, None, tp)
    placed = (
        split,
        split,
        split,
        split,
        split,
        P(),
        P(tp),
        P(ctx, None, None),
        P(ctx, None, None),
        split,
        split,
        split,
    )
    return jax.shard_map(
        on_device,
        mesh=fine,
        in_specs=placed,
        out_specs=(split, split),
        check_vma=False,
    )
```
